128 devices in a mesh: row: 32 (over y_lo, z, x), col: 4 (over y_hi, core).
Axes of the slice: x: 4, y: 4 (y_hi: 2, y_lo: 2; y = y_hi * 2 + y_lo), z: 4, core: 2. Of those that a mesh axis runs over, the one named last changes fastest.
Arguments:
- image: bfloat16 [18432, 1152], P(('row', 'col')), may hold values from -6 to 6
- text: bfloat16 [18432, 1152], P(('col', 'row')), may hold values from -6 to 6
- log_scale: float32 [], replicated, may hold values from 0.9 to 1.3
Outputs:
- loss_value: float32 [], replicated
- image_grad: float32 [18432, 1152], P(('row', 'col'))
- text_grad: float32 [18432, 1152], P(('col', 'row'))
The draws below stay inside these ranges and needn't reach their ends.
All inputs are finite; a program needn't handle non-finite values.
Results may differ from the reference program's by a relative error of at most 0.00175.
Values may be sent and summed in bfloat16 or wider, within the bound.
No kernel may reach another device: no remote copies, remote signals or barrier semaphores. Data moves between devices by JAX's collectives and lax.ppermute only.
A program may use at most 128 MiB of HBM per device.

```python
import jax
import jax.numpy as jnp
from jax import lax

D = 1152
ROWS = 18432
N_ROW = 32


def paired_draw(key):
    keys = jax.random.split(key, 5)
    base_scale = D ** (-0.25)
    first_part = jax.random.normal(keys[0], (ROWS, D), jnp.float32)
    second_part = jax.random.normal(keys[1], (ROWS, D), jnp.float32)
    image_scale = jnp.exp(jax.random.uniform(keys[3], (ROWS, 1), jnp.float32, -1.05, 1.25))
    text_scale = jnp.exp(jax.random.uniform(keys[4], (ROWS, 1), jnp.float32, -1.05, 1.25))
    image_rows = first_part * base_scale * image_scale
    text_rows = (0.1 * first_part + 0.995 * second_part) * base_scale * text_scale
    return (jnp.clip(image_rows, -6.0, 6.0), jnp.clip(text_rows, -6.0, 6.0))


def draw_image(key, part):
    return paired_draw(key)[0].astype(jnp.bfloat16)


def draw_text(key, part):
    return paired_draw(key)[1].astype(jnp.bfloat16)


def setup_inputs(seed: int = 0) -> dict:
    arg_keys = jax.random.split(jax.random.key(seed), 4)
    return {
        "image": draw_image(jax.random.fold_in(arg_keys[3], 71), 0),
        "text": draw_text(jax.random.fold_in(arg_keys[3], 71), 0),
        "log_scale": jnp.clip(jax.random.uniform(arg_keys[2], (), jnp.float32, 0.9, 1.3), 0.9, 1.3),
    }


def reference(image, text, log_scale):
    inverse_temp = jnp.exp(log_scale)
    total_rows = image.shape[0]
    block_rows = total_rows // N_ROW
    image_blocks = image.reshape(N_ROW, block_rows, image.shape[1])
    block_ids = jnp.arange(N_ROW, dtype=jnp.int32)
    col_ids = jnp.arange(total_rows, dtype=jnp.int32)

    def first_pass(state_pair, inputs):
        image_part, block_id = inputs
        scores = inverse_temp * jnp.dot(image_part, text.T, preferred_element_type=jnp.float32)
        row_peak = jnp.max(scores, axis=1)
        row_lse = row_peak + jnp.log(jnp.sum(jnp.exp(scores - row_peak[:, None]), axis=1))
        col_top, col_total = state_pair
        new_top = jnp.maximum(col_top, jnp.max(scores, axis=0))
        col_total = col_total * jnp.exp(col_top - new_top) + jnp.sum(jnp.exp(scores - new_top[None, :]), axis=0)
        row_ids = block_id * block_rows + jnp.arange(block_rows, dtype=jnp.int32)
        matches = row_ids[:, None] == col_ids[None, :]
        diagonal_sum = jnp.sum(jnp.where(matches, scores, jnp.float32(0.0)))
        return (new_top, col_total), (row_lse, diagonal_sum)

    start_pair = (jnp.full((total_rows,), -jnp.inf, jnp.float32), jnp.zeros((total_rows,), jnp.float32))
    (col_top, col_total), (row_lse, diagonal_sums) = lax.scan(first_pass, start_pair, (image_blocks, block_ids))
    col_lse = col_top + jnp.log(col_total)
    row_lse = row_lse.reshape(total_rows)
    loss_value = (jnp.sum(row_lse) + jnp.sum(col_lse) - 2.0 * jnp.sum(diagonal_sums)) / (2.0 * total_rows)
    row_lse_blocks = row_lse.reshape(N_ROW, block_rows)

    def second_pass(text_accum, inputs):
        image_part, block_id, lse_part = inputs
        scores = inverse_temp * jnp.dot(image_part, text.T, preferred_element_type=jnp.float32)
        row_ids = block_id * block_rows + jnp.arange(block_rows, dtype=jnp.int32)
        matches = (row_ids[:, None] == col_ids[None, :]).astype(jnp.float32)
        weights = (0.5 * (jnp.exp(scores - lse_part[:, None]) + jnp.exp(scores - col_lse[None, :])) - matches).astype(jnp.bfloat16)
        image_part_grad = inverse_temp * jnp.dot(weights, text, preferred_element_type=jnp.float32)
        text_accum = text_accum + inverse_temp * jnp.dot(weights.T, image_part, preferred_element_type=jnp.float32)
        return text_accum, image_part_grad

    text_grad, image_grad = lax.scan(second_pass, jnp.zeros(text.shape, jnp.float32), (image_blocks, block_ids, row_lse_blocks))
    return loss_value, image_grad.reshape(image.shape), text_grad
```

```python
import jax
import jax.numpy as jnp
from jax import lax
from jax.sharding import Mesh, PartitionSpec as P

AXES = ("ylo", "z", "x", "yhi", "core")
RING = 4


def ring_shift(value, axis, step):
    return lax.ppermute(value, axis, [(i, (i + step) % RING) for i in range(RING)])


def swap(value, axis):
    return lax.ppermute(value, axis, [(0, 1), (1, 0)])


def merge(pairs):
    top = pairs[0][0]
    for pair in pairs[1:]:
        top = jnp.maximum(top, pair[0])
    total = sum(pair[1] * jnp.exp(pair[0] - top) for pair in pairs)
    return jnp.stack([top, total])


def ring_merge(stat, axis):
    pairs = [stat]
    for step in range(1, RING):
        pairs.append(jnp.roll(ring_shift(stat, axis, step), step, axis=1))
    return merge(pairs)


def on_device(image, text, log_scale):
    inverse_temp = jnp.exp(log_scale)
    rows, width = image.shape
    place = {a: lax.axis_index(a) for a in AXES}

    text_far = swap(text, "ylo")
    image_far = swap(image, "yhi")
    text_slots = {(0, 0): text, (0, 1): text_far}
    image_slots = {(0, 0): image, (0, 1): image_far}
    for h in range(2):
        for step in (1, 3, 2):
            text_slots[step, h] = ring_shift(text_slots[0, h], "z", step)
            image_slots[step, h] = ring_shift(image_slots[0, h], "x", step)
    image_near = jnp.concatenate([image_slots[d, h] for h in range(2) for d in range(RING)])
    image_block = jnp.concatenate([image_near, swap(image_near, "core")])
    text_block = jnp.concatenate([text_slots[d, h] for h in range(2) for d in range(RING)])

    back = jnp.arange(RING, dtype=jnp.int32)
    pair = jnp.arange(2, dtype=jnp.int32)
    x_of = (place["x"] - back) % RING
    z_of = (place["z"] - back) % RING
    yhi_of = place["yhi"] ^ pair
    ylo_of = place["ylo"] ^ pair
    core_of = place["core"] ^ pair
    image_ids = (((place["ylo"] * 4 + place["z"]) * 4 + x_of[None, None, :]) * 4
                 + yhi_of[None, :, None] * 2 + core_of[:, None, None]).reshape(-1)
    text_ids = ((place["yhi"] * 2 + place["core"]) * 32
                + (ylo_of[:, None] * 4 + z_of[None, :]) * 4 + place["x"]).reshape(-1)
    within = jnp.arange(rows, dtype=jnp.int32)
    row_ids = (image_ids[:, None] * rows + within).reshape(-1)
    col_ids = (text_ids[:, None] * rows + within).reshape(-1)

    scores = inverse_temp * lax.dot_general(
        image_block, text_block, (((1,), (1,)), ((), ())), preferred_element_type=jnp.float32
    )
    row_top = jnp.max(scores, axis=1)
    col_top = jnp.max(scores, axis=0)
    row_total = jnp.sum(jnp.exp(scores - row_top[:, None]), axis=1)
    col_total = jnp.sum(jnp.exp(scores - col_top[None, :]), axis=0)
    matches = row_ids[:, None] == col_ids[None, :]
    diagonal_sum = jnp.sum(jnp.where(matches, scores, jnp.float32(0.0)))

    row_stat = jnp.stack([row_top, row_total]).reshape(2, 2, 2, RING, rows).transpose(0, 3, 1, 2, 4)
    col_stat = jnp.stack([col_top, col_total]).reshape(2, 2, RING, rows).transpose(0, 2, 1, 3)
    row_stat = ring_merge(row_stat, "x")
    col_stat = ring_merge(col_stat, "z")
    row_stat = merge([row_stat, swap(row_stat, "yhi")[:, :, :, ::-1]])
    col_stat = merge([col_stat, swap(col_stat, "ylo")[:, :, ::-1]])
    row_stat = merge([row_stat, swap(row_stat, "core")[:, :, ::-1]])
    row_lse = (row_stat[0] + jnp.log(row_stat[1])).transpose(1, 2, 0, 3).reshape(-1)
    col_lse = (col_stat[0] + jnp.log(col_stat[1])).transpose(1, 0, 2).reshape(-1)

    total_rows = rows * 128
    local_loss = jnp.sum(row_lse[:rows]) + jnp.sum(col_lse[:rows]) - 2.0 * diagonal_sum
    loss_value = lax.psum(local_loss, AXES) / (2.0 * total_rows)

    weights = (
        0.5 * (jnp.exp(scores - row_lse[:, None]) + jnp.exp(scores - col_lse[None, :]))
        - matches.astype(jnp.float32)
    ).astype(jnp.bfloat16)

    half = RING * rows

    def image_part(lo):
        return jnp.dot(weights[lo:lo + half], text_block, preferred_element_type=jnp.float32)

    def text_part(lo):
        return lax.dot_general(
            weights[:, lo:lo + half], image_block, (((0,), (0,)), ((), ())), preferred_element_type=jnp.float32
        )

    def ring_sum(part, axis):
        part16 = part.astype(jnp.float16)
        total = part[:rows]
        for step in range(1, RING):
            total = total + ring_shift(part16[step * rows:(step + 1) * rows], axis, -step).astype(jnp.float32)
        return total

    text_far_sum = ring_sum(text_part(half), "z")
    image_other = [image_part(2 * half + half * h).astype(jnp.float16) for h in (1, 0)]
    image_far_part = image_part(half) + swap(image_other[0], "core").astype(jnp.float32)
    image_far_sum = ring_sum(image_far_part, "x")
    image_near_part = image_part(0) + swap(image_other[1], "core").astype(jnp.float32)
    image_grad = ring_sum(image_near_part, "x") + swap(image_far_sum.astype(jnp.float16), "yhi").astype(jnp.float32)
    text_grad = ring_sum(text_part(0), "z") + swap(text_far_sum.astype(jnp.float16), "ylo").astype(jnp.float32)
    return loss_value, inverse_temp * image_grad, inverse_temp * text_grad


def solution(mesh):
    fine = Mesh(mesh.devices.reshape(2, 4, 4, 2, 2), AXES)
    in_specs = (P(AXES, None), P(("yhi", "core", "ylo", "z", "x"), None), P())
    out_specs = (P(), P(AXES, None), P(("yhi", "core", "ylo", "z", "x"), None))
    return jax.shard_map(
        on_device, mesh=fine, in_specs=in_specs, out_specs=out_specs, check_vma=False
    )
```

```python
import math

import jax
import jax.numpy as jnp
from jax import lax
from jax.experimental import pallas as pl
from jax.experimental.pallas import tpu as pltpu
from jax.sharding import Mesh, PartitionSpec as P

AXES = ("ylo", "z", "x", "yhi", "core")
RING = 4
TILE_SLOTS = 2


def ring_shift(value, axis, step):
    return lax.ppermute(value, axis, [(i, (i + step) % RING) for i in range(RING)])


def ring_split(value, axis, sign):
    pairs = []
    for i in range(RING):
        for core in range(2):
            target = (i + (sign if core == 0 else -sign)) % RING
            pairs.append((i * 2 + core, target * 2 + core))
    return lax.ppermute(value, (axis, "core"), pairs)


def swap(value, axis):
    return lax.ppermute(value, axis, [(0, 1), (1, 0)])


def ring_gather(value, axis, core):
    one = ring_shift(value, axis, 1)
    three = ring_shift(value, axis, 3)
    two = ring_split(jnp.where(core == 0, one, three), axis, 1)
    return [value, one, two, three]


def merge(pairs):
    top = pairs[0][0]
    for pair in pairs[1:]:
        top = jnp.maximum(top, pair[0])
    total = sum(pair[1] * jnp.exp2(pair[0] - top) for pair in pairs)
    return jnp.stack([top, total])


def ring_merge(stat, axis):
    pairs = [stat]
    for step in (1, 3, 2):
        pairs.append(jnp.roll(ring_shift(stat, axis, step), step, axis=1))
    return merge(pairs)


def to_lanes(column):
    n = column.shape[0]
    return jnp.broadcast_to(column, (n, 128)).T[0:1, :]


def score_kernel(image_sizes, text_sizes, rows, scale_ref, ids_ref, col_ids_ref, *refs):
    n_image, n_text = len(image_sizes), len(text_sizes)
    image_refs, refs = refs[:n_image], refs[n_image:]
    text_refs, refs = refs[:n_text], refs[n_text:]
    keep_text = n_text > 1
    scores_ref, held_image_ref = refs[:2]
    refs = refs[2:]
    if keep_text:
        held_text_ref, refs = refs[0], refs[1:]
    row_ref, col_ref, diag_ref, x_ref, t_ref, s_ref, in_sem, out_sem = refs

    def copies_in(sources, sizes, target, base):
        at, out = 0, []
        for k, (source, size) in enumerate(zip(sources, sizes)):
            out.append((at, pltpu.make_async_copy(source, target.at[pl.ds(at, size)], in_sem.at[base + k])))
            at += size
        return out

    text_in = copies_in(text_refs, text_sizes, t_ref, 0)
    image_in = copies_in(image_refs, image_sizes, x_ref, n_text)
    for _, copy in text_in + image_in:
        copy.start()
    for _, copy in text_in:
        copy.wait()
    out = []
    if keep_text:
        out.append(pltpu.make_async_copy(t_ref, held_text_ref, out_sem.at[0]))
        out[-1].start()

    total_rows = x_ref.shape[0]
    tile = rows * TILE_SLOTS
    scale = scale_ref[0]
    col_parts = []
    diag = jnp.zeros((1, t_ref.shape[0]), jnp.float32)
    for i in range(total_rows // tile):
        lo = i * tile
        while image_in and image_in[0][0] < lo + tile:
            image_in.pop(0)[1].wait()
        s_ref[pl.ds(lo, tile), :] = scale * lax.dot_general(
            x_ref[pl.ds(lo, tile), :], t_ref[...], (((1,), (1,)), ((), ())), preferred_element_type=jnp.float32
        )
        copy = pltpu.make_async_copy(s_ref.at[pl.ds(lo, tile)], scores_ref.at[pl.ds(lo, tile)], out_sem.at[2 + i])
        copy.start()
        out.append(copy)
        s = s_ref[pl.ds(lo, tile), :]
        col_top = jnp.max(s, axis=0, keepdims=True)
        col_parts.append((col_top, jnp.sum(jnp.exp2(s - col_top), axis=0, keepdims=True)))
        for j in range(TILE_SLOTS):
            slot = i * TILE_SLOTS + j
            s = s_ref[pl.ds(slot * rows, rows), :]
            row_top = jnp.max(s, axis=1, keepdims=True)
            row_sum = jnp.sum(jnp.exp2(s - row_top), axis=1, keepdims=True)
            row_ref[0, pl.ds(slot, 1), :] = to_lanes(row_top)
            row_ref[1, pl.ds(slot, 1), :] = to_lanes(row_sum)
            ids = ids_ref[slot] + lax.broadcasted_iota(jnp.int32, (rows, 1), 0)
            diag = diag + jnp.sum(jnp.where(ids == col_ids_ref[...], s, 0.0), axis=0, keepdims=True)
    copy = pltpu.make_async_copy(x_ref, held_image_ref, out_sem.at[1])
    copy.start()
    out.append(copy)
    top = col_parts[0][0]
    for part in col_parts[1:]:
        top = jnp.maximum(top, part[0])
    col_ref[0:1, :] = top
    col_ref[1:2, :] = sum(part[1] * jnp.exp2(part[0] - top) for part in col_parts)
    diag_ref[...] = diag
    for copy in out:
        copy.wait()


def score_call(images, texts, scale, ids, col_ids, rows, name):
    width = images[0].shape[1]
    image_sizes = [a.shape[0] for a in images]
    text_sizes = [a.shape[0] for a in texts]
    m, n = sum(image_sizes), sum(text_sizes)
    slots = m // rows
    keep_text = len(texts) > 1
    hbm = pl.BlockSpec(memory_space=pl.ANY)
    vmem = pl.BlockSpec(memory_space=pltpu.VMEM)
    smem = pl.BlockSpec(memory_space=pltpu.SMEM)
    held = [jax.ShapeDtypeStruct((m, width), jnp.bfloat16)]
    if keep_text:
        held.append(jax.ShapeDtypeStruct((n, width), jnp.bfloat16))

    def kernel(*refs):
        score_kernel(image_sizes, text_sizes, rows, *refs)

    return pl.pallas_call(
        kernel,
        in_specs=[smem, smem, vmem] + [hbm] * (len(images) + len(texts)),
        out_specs=[hbm] * (1 + len(held)) + [vmem] * 3,
        out_shape=[jax.ShapeDtypeStruct((m, n), jnp.float32)] + held + [
            jax.ShapeDtypeStruct((2, slots, rows), jnp.float32),
            jax.ShapeDtypeStruct((2, n), jnp.float32),
            jax.ShapeDtypeStruct((1, n), jnp.float32),
        ],
        scratch_shapes=[
            pltpu.VMEM((m, width), jnp.bfloat16),
            pltpu.VMEM((n, width), jnp.bfloat16),
            pltpu.VMEM((m, n), jnp.float32),
            pltpu.SemaphoreType.DMA((len(images) + len(texts),)),
            pltpu.SemaphoreType.DMA((2 + slots // TILE_SLOTS,)),
        ],
        compiler_params=pltpu.CompilerParams(vmem_limit_bytes=40 * 1024 * 1024),
        cost_estimate=pl.CostEstimate(
            flops=2 * m * n * width, bytes_accessed=4 * m * n + 4 * (m + n) * width, transcendentals=2 * m * n
        ),
        name=name,
    )(scale, ids, col_ids, *images, *texts)


def total_over_devices(value):
    for axis in ("core", "yhi", "ylo"):
        value = value + swap(value, axis)
    for axis in ("x", "z"):
        value = value + ring_shift(value, axis, 1)
        value = value + ring_shift(value, axis, 2)
    return value


def on_device(image, text, log_scale):
    inverse_temp = jnp.exp(log_scale)
    rows = image.shape[0]
    half = RING * rows
    core = lax.axis_index("core")

    text_far = swap(text, "ylo")
    image_far = swap(image, "yhi")
    text_near_slots = ring_gather(text, "z", core)
    image_near_slots = ring_gather(image, "x", core)
    text_far_slots = ring_gather(text_far, "z", core)
    image_far_slots = ring_gather(image_far, "x", core)
    image_near_other = swap(jnp.concatenate(image_near_slots), "core")
    image_far_other = [swap(a, "core") for a in image_far_slots]

    back = jnp.arange(RING, dtype=jnp.int32)
    pair = jnp.arange(2, dtype=jnp.int32)
    x_of = (lax.axis_index("x") - back) % RING
    z_of = (lax.axis_index("z") - back) % RING
    yhi_of = lax.axis_index("yhi") ^ pair
    ylo_of = lax.axis_index("ylo") ^ pair
    core_of = core ^ pair
    image_ids = (((lax.axis_index("ylo") * 4 + lax.axis_index("z")) * 4 + x_of[None, None, :]) * 4
                 + yhi_of[:, None, None] * 2 + core_of[None, :, None]).reshape(2, 2 * RING)
    text_ids = ((lax.axis_index("yhi") * 2 + core) * 32
                + (ylo_of[:, None] * 4 + z_of[None, :]) * 4 + lax.axis_index("x")).reshape(-1)
    within = jnp.arange(rows, dtype=jnp.int32)
    col_ids = (text_ids[:, None] * rows + within).reshape(1, -1)

    scale = (inverse_temp * jnp.float32(math.log2(math.e))).reshape(1)
    s_near, x_near, t_all, row_near, col_near, diag_near = score_call(
        image_near_slots + [image_near_other], text_near_slots + text_far_slots,
        scale, image_ids[0] * rows, col_ids, rows, "score_near")
    s_far, x_far, row_far, col_far, diag_far = score_call(
        image_far_slots + image_far_other, [t_all],
        scale, image_ids[1] * rows, col_ids, rows, "score_far")
    diagonal = jnp.sum(diag_near) + jnp.sum(diag_far)

    row_stat = jnp.stack([row_near, row_far], axis=1).reshape(2, 2, 2, RING, rows).transpose(0, 3, 1, 2, 4)
    col_stat = merge([col_near, col_far]).reshape(2, 2, RING, rows).transpose(0, 2, 1, 3)
    row_stat = ring_merge(row_stat, "x")
    col_stat = ring_merge(col_stat, "z")
    row_stat = merge([row_stat, swap(row_stat, "yhi")[:, :, ::-1]])
    col_stat = merge([col_stat, swap(col_stat, "ylo")[:, :, ::-1]])
    row_stat = merge([row_stat, swap(row_stat, "core")[:, :, :, ::-1]])
    row_lse = (row_stat[0] + jnp.log2(row_stat[1])).transpose(1, 2, 0, 3).reshape(2, -1)
    col_lse = (col_stat[0] + jnp.log2(col_stat[1])).transpose(1, 0, 2).reshape(-1)

    def weights_of(s, lse, ids):
        row_ids = (ids[:, None] * rows + within).reshape(-1)
        matches = row_ids[:, None] == col_ids
        return (
            0.5 * (jnp.exp2(s - lse[:, None]) + jnp.exp2(s - col_lse[None, :])) - matches.astype(jnp.float32)
        ).astype(jnp.bfloat16)

    w_far = weights_of(s_far, row_lse[1], image_ids[1])
    w_near = weights_of(s_near, row_lse[0], image_ids[0])

    def image_part(w, lo):
        return jnp.dot(w[lo:lo + half], t_all, preferred_element_type=jnp.float32)

    def text_part(lo):
        dims = (((0,), (0,)), ((), ()))
        return (lax.dot_general(w_far[:, lo:lo + half], x_far, dims, preferred_element_type=jnp.float32)
                + lax.dot_general(w_near[:, lo:lo + half], x_near, dims, preferred_element_type=jnp.float32))

    def ring_sum(part, axis):
        slots = part.reshape(RING, rows, -1)
        through = ring_split(slots[2].astype(jnp.float16), axis, -1).astype(jnp.float32)
        right = slots[3] + jnp.where(core == 0, 0.0, through)
        left = slots[1] + jnp.where(core == 0, through, 0.0)
        return (slots[0] + ring_shift(left.astype(jnp.float16), axis, -1).astype(jnp.float32)
                + ring_shift(right.astype(jnp.float16), axis, 1).astype(jnp.float32))

    far_other = swap(image_part(w_far, half).astype(jnp.float16), "core")
    image_far_sum = ring_sum(image_part(w_far, 0) + far_other.astype(jnp.float32), "x")
    text_far_sum = ring_sum(text_part(half), "z")
    near_other = swap(image_part(w_near, half).astype(jnp.float16), "core")
    image_near_sum = ring_sum(image_part(w_near, 0) + near_other.astype(jnp.float32), "x")
    text_near_sum = ring_sum(text_part(0), "z")
    image_grad = image_near_sum + swap(image_far_sum.astype(jnp.float16), "yhi").astype(jnp.float32)
    text_grad = text_near_sum + swap(text_far_sum.astype(jnp.float16), "ylo").astype(jnp.float32)

    total_rows = rows * 128
    local = jnp.sum(row_lse[0, :rows]) + jnp.sum(col_lse[:rows]) - 2.0 * diagonal
    loss_value = total_over_devices(local * jnp.float32(math.log(2.0))) / (2.0 * total_rows)
    return loss_value, inverse_temp * image_grad, inverse_temp * text_grad


def solution(mesh):
    fine = Mesh(mesh.devices.reshape(2, 4, 4, 2, 2), AXES)
    text_spec = P(("yhi", "core", "ylo", "z", "x"), None)
    return jax.shard_map(
        on_device, mesh=fine, in_specs=(P(AXES, None), text_spec, P()),
        out_specs=(P(), P(AXES, None), text_spec), check_vma=False
    )
```

```python
import math

import jax
import jax.numpy as jnp
from jax import lax
from jax.experimental import pallas as pl
from jax.experimental.pallas import tpu as pltpu
from jax.sharding import Mesh, PartitionSpec as P

AXES = ("ylo", "z", "x", "yhi", "core")
RING = 4
TILE_SLOTS = 2
VMEM_LIMIT = 12 * 1024 * 1024


def f32(*shape):
    return jax.ShapeDtypeStruct(shape, jnp.float32)


def bf16(*shape):
    return jax.ShapeDtypeStruct(shape, jnp.bfloat16)


def vmem_call(kernel, out_shape, name, flops, transcendentals, scalars, *args):
    vmem = pl.BlockSpec(memory_space=pltpu.VMEM)
    nbytes = sum(a.size * a.dtype.itemsize for a in args)
    nbytes += sum(math.prod(o.shape) * o.dtype.itemsize for o in out_shape)
    return pl.pallas_call(
        kernel,
        in_specs=[pl.BlockSpec(memory_space=pltpu.SMEM)] * len(scalars) + [vmem] * len(args),
        out_specs=[vmem] * len(out_shape),
        out_shape=out_shape,
        compiler_params=pltpu.CompilerParams(vmem_limit_bytes=VMEM_LIMIT),
        cost_estimate=pl.CostEstimate(flops=flops, bytes_accessed=nbytes, transcendentals=transcendentals),
        name=name,
    )(*scalars, *args)


def to_lanes(column):
    return jnp.broadcast_to(column, (column.shape[0], 128)).T[0:1, :]


def to_rows(line):
    return jnp.broadcast_to(line, (128, line.shape[1])).T[:, 0:1]


def merge(stats):
    top = stats[0][0]
    for stat in stats[1:]:
        top = jnp.maximum(top, stat[0])
    total = sum(stat[1] * jnp.exp2(stat[0] - top) for stat in stats)
    return [top, total] + [sum(stat[k] for stat in stats) for k in range(2, len(stats[0]))]


def score_call(images, texts, scale, pairs, near_stats, rows, name):
    width = images[0].shape[1]
    sizes = [a.shape[0] for a in images]
    text_sizes = [a.shape[0] for a in texts]
    m, n = sum(sizes), sum(text_sizes)
    slots = m // rows
    before = near_stats[0].shape[1] if near_stats else 0
    keep_text = len(texts) > 1

    def kernel(scale_ref, pairs_ref, *refs):
        image_refs, refs = refs[:len(images)], refs[len(images):]
        text_refs, refs = refs[:len(texts)], refs[len(texts):]
        held, refs = refs[:len(near_stats)], refs[len(near_stats):]
        s_ref, x_ref, row_ref, col_ref = refs[:4]
        t_ref = refs[4] if keep_text else text_refs[0]

        def fill(target, sources, counts):
            at = 0
            for source, count in zip(sources, counts):
                target[pl.ds(at, count), :] = source[...]
                at += count

        if keep_text:
            fill(t_ref, text_refs, text_sizes)
        fill(x_ref, image_refs, sizes)
        tile = rows * TILE_SLOTS
        tiles = m // tile
        scale = scale_ref[0]
        col_parts = []

        def scores(i):
            s_ref[pl.ds(i * tile, tile), :] = scale * lax.dot_general(
                x_ref[pl.ds(i * tile, tile), :], t_ref[...], (((1,), (1,)), ((), ())),
                preferred_element_type=jnp.float32)

        def stats(i):
            s = s_ref[pl.ds(i * tile, tile), :]
            col_top = jnp.max(s, axis=0, keepdims=True)
            col_parts.append((col_top, jnp.sum(jnp.exp2(s - col_top), axis=0, keepdims=True)))
            for j in range(TILE_SLOTS):
                slot = i * TILE_SLOTS + j
                s = s_ref[pl.ds(slot * rows, rows), :]
                row_top = jnp.max(s, axis=1, keepdims=True)
                row_sum = jnp.sum(jnp.exp2(s - row_top), axis=1, keepdims=True)
                row_ref[0, pl.ds(before + slot, 1), :] = to_lanes(row_top)
                row_ref[1, pl.ds(before + slot, 1), :] = to_lanes(row_sum)

        scores(0)
        for i in range(tiles):
            if i + 1 < tiles:
                scores(i + 1)
            stats(i)
        top, total = merge(col_parts)
        for k in range(n // rows):
            at = slice(k * rows, (k + 1) * rows)
            part = [(top[:, at], total[:, at])]
            if held:
                part.append((held[1][0, pl.ds(k, 1), :], held[1][1, pl.ds(k, 1), :]))
            col_ref[0, pl.ds(k, 1), :], col_ref[1, pl.ds(k, 1), :] = merge(part)
        if held:
            row_ref[:, pl.ds(0, before), :] = held[0][...]
        row_ref[2, pl.ds(before, slots), :] = jnp.zeros((slots, rows), jnp.float32)
        for slot in range(slots):
            for k in range(n // rows):
                @pl.when(pairs_ref[slot] == k)
                def _():
                    s = s_ref[pl.ds(slot * rows, rows), :][:, k * rows:(k + 1) * rows]
                    mask = (lax.broadcasted_iota(jnp.int32, (rows, 1), 0)
                            == lax.broadcasted_iota(jnp.int32, (1, rows), 1))
                    row_ref[2, pl.ds(before + slot, 1), :] = jnp.sum(jnp.where(mask, s, 0.0), axis=0, keepdims=True)

    out_shape = [f32(m, n), bf16(m, width), f32(3, before + slots, rows), f32(2, n // rows, rows)]
    out_shape += [bf16(n, width)] * keep_text
    return vmem_call(kernel, out_shape, name, 2 * m * n * width, 2 * m * n, [scale, pairs],
                     *images, *texts, *near_stats)


def turned(ref, k, step):
    rings = []
    for lo in range(0, ref.shape[1], RING):
        rings.append(ref[k, pl.ds(lo + RING - step, step), :])
        rings.append(ref[k, pl.ds(lo, RING - step), :])
    return jnp.concatenate(rings, axis=0)


def swapped(ref, k, group):
    parts = []
    for lo in range(0, ref.shape[1], 2 * group):
        parts.append(ref[k, pl.ds(lo + group, group), :])
        parts.append(ref[k, pl.ds(lo, group), :])
    return jnp.concatenate(parts, axis=0)


def ring_merge_call(row, rows_in, col, cols_in):
    def kernel(*refs):
        row_refs, col_refs = refs[:RING], refs[RING:2 * RING]
        for own, out in ((row_refs, refs[-2]), (col_refs, refs[-1])):
            planes = out.shape[0]
            stats = [[own[0][k] for k in range(planes)]]
            for step in range(1, RING):
                stats.append([turned(own[step], k, step) for k in range(planes)])
            for k, value in enumerate(merge(stats)):
                out[k] = value

    return vmem_call(kernel, [f32(*row.shape), f32(*col.shape)], "merge_ring", 0, 0, [],
                     row, *rows_in, col, *cols_in)


def pair_merge_call(row, row_in, col, col_in):
    half = col.shape[1] // 2

    def kernel(row_ref, row_in_ref, col_ref, col_in_ref, row_out, lse_ref, loss_ref):
        planes = range(row_ref.shape[0])
        for k, value in enumerate(merge([
                [row_ref[k] for k in planes], [swapped(row_in_ref, k, row_ref.shape[1] // 2) for k in planes]])):
            row_out[k] = value
        top, total = merge([[col_ref[k] for k in range(2)], [swapped(col_in_ref, k, half) for k in range(2)]])
        lse = top + jnp.log2(total)
        lse_ref[...] = lse
        loss_ref[...] = jnp.sum(lse, axis=0, keepdims=True)

    return vmem_call(kernel, [f32(*row.shape), f32(*col.shape[1:]), f32(1, col.shape[2])], "merge_pair", 0, 0, [],
                     row, row_in, col, col_in)


def core_merge_call(row, row_in):
    def kernel(row_ref, row_in_ref, lse_ref, loss_ref):
        planes = range(row_ref.shape[0])
        top, total, own = merge([[row_ref[k] for k in planes], [swapped(row_in_ref, k, RING) for k in planes]])
        lse = top + jnp.log2(total)
        lse_ref[...] = lse
        loss_ref[...] = jnp.sum(lse - 2.0 * own, axis=0, keepdims=True)

    return vmem_call(kernel, [f32(*row.shape[1:]), f32(1, row.shape[2])], "merge_core", 0, 0, [], row, row_in)


def soft_weights(v, row_lse, col_lse, first_id, col_ids):
    ids = first_id + lax.broadcasted_iota(jnp.int32, (v.shape[0], 1), 0)
    soft = 0.5 * (jnp.exp2(v - to_rows(row_lse)) + jnp.exp2(v - col_lse))
    return (soft - jnp.where(ids == col_ids, 1.0, 0.0)).astype(jnp.bfloat16)


def weight_steps(w_ref, s_ref, row_ref, col_ref, ids_ref, col_ids_ref, first, rows):
    col_lse = jnp.concatenate([col_ref[pl.ds(k, 1), :] for k in range(col_ref.shape[0])], axis=1)

    def weights(i):
        for j in range(TILE_SLOTS):
            slot = i * TILE_SLOTS + j
            at = pl.ds(slot * rows, rows)
            w_ref[at, :] = soft_weights(
                s_ref[at, :], row_ref[pl.ds(first + slot, 1), :], col_lse, ids_ref[slot], col_ids_ref[...])

    return weights


def image_call(s, row_lse, first, col_lse, ids, col_ids, text, rows, name):
    m, n = s.shape
    width = text.shape[1]
    half = m // 2

    def kernel(ids_ref, s_ref, row_ref, col_ref, col_ids_ref, t_ref, w_ref, own_ref, other_ref):
        tile = rows * TILE_SLOTS
        tiles = m // tile
        weights = weight_steps(w_ref, s_ref, row_ref, col_ref, ids_ref, col_ids_ref, first, rows)

        def dots(i):
            out = own_ref if i * tile < half else other_ref
            out[pl.ds(i * tile % half, tile), :] = jnp.dot(
                w_ref[pl.ds(i * tile, tile), :], t_ref[...], preferred_element_type=jnp.float32)

        weights(0)
        for i in range(tiles):
            if i + 1 < tiles:
                weights(i + 1)
            dots(i)

    return vmem_call(kernel, [bf16(m, n), f32(half, width), f32(half, width)], name, 2 * m * n * width, 2 * m * n,
                     [ids], s, row_lse, col_lse, col_ids, text)


def text_call(s, row_lse, first, col_lse, ids, col_ids, x_near, w_far, x_far, rows, name):
    m, n = s.shape
    width = x_near.shape[1]
    chunk = 384

    def kernel(ids_ref, s_ref, row_ref, col_ref, col_ids_ref, xn_ref, wf_ref, xf_ref, w_ref, part_ref):
        tiles = m // (rows * TILE_SLOTS)
        dims = (((0,), (0,)), ((), ()))
        weights = weight_steps(w_ref, s_ref, row_ref, col_ref, ids_ref, col_ids_ref, first, rows)
        weights(0)
        for j in range(width // chunk):
            at = pl.ds(j * chunk, chunk)
            part_ref[:, at] = lax.dot_general(wf_ref[...], xf_ref[:, at], dims, preferred_element_type=jnp.float32)
            if j + 1 < tiles:
                weights(j + 1)
        for j in range(width // chunk):
            at = pl.ds(j * chunk, chunk)
            part_ref[:, at] += lax.dot_general(w_ref[...], xn_ref[:, at], dims, preferred_element_type=jnp.float32)

    return vmem_call(kernel, [bf16(m, n), f32(n, width)], name, 4 * m * n * width, 2 * m * n,
                     [ids], s, row_lse, col_lse, col_ids, x_near, w_far, x_far)


def near_call(w, text, name):
    m, n = w.shape
    width = text.shape[1]
    half = m // 2

    def kernel(w_ref, t_ref, own_ref, other_ref):
        other_ref[...] = jnp.dot(w_ref[half:, :], t_ref[...], preferred_element_type=jnp.float32)
        own_ref[...] = jnp.dot(w_ref[:half, :], t_ref[...], preferred_element_type=jnp.float32)

    return vmem_call(kernel, [f32(half, width), f32(half, width)], name, 2 * m * n * width, 0, [], w, text)


def after(value, *others):
    return lax.optimization_barrier((value, *others))[0]


def ring_shift(value, axis, step):
    return lax.ppermute(value, axis, [(i, (i + step) % RING) for i in range(RING)])


def ring_split(value, axis, sign):
    pairs = []
    for i in range(RING):
        for core in range(2):
            target = (i + (sign if core == 0 else -sign)) % RING
            pairs.append((i * 2 + core, target * 2 + core))
    return lax.ppermute(value, (axis, "core"), pairs)


def swap(value, axis):
    return lax.ppermute(value, axis, [(0, 1), (1, 0)])


def ring_gather(value, axis, core, wait_for=None):
    one = ring_shift(value, axis, 1)
    three = ring_shift(value if wait_for is None else after(value, wait_for), axis, 3)
    two = ring_split(jnp.where(core == 0, one, three), axis, 1)
    return [value, one, two, three]


def ring_total(value, axis):
    value = value + ring_shift(value, axis, 1)
    return value, lambda held: held + ring_shift(held, axis, 2)


def summed(own, other):
    return own + other.astype(jnp.float32)


def ring_outgoing(one, three, through, core):
    through = through.astype(jnp.float32)
    left = one + jnp.where(core == 0, through, 0.0)
    right = three + jnp.where(core == 0, 0.0, through)
    return left.astype(jnp.float16), right.astype(jnp.float16)


def ring_arrived(own, left, right, axis):
    return own + ring_shift(left, axis, -1).astype(jnp.float32) + ring_shift(right, axis, 1).astype(jnp.float32)


def on_device(image, text, log_scale):
    inverse_temp = jnp.exp(log_scale)
    rows = image.shape[0]
    half = RING * rows
    core = lax.axis_index("core")

    text_far = swap(text, "ylo")
    image_far = swap(image, "yhi")
    image_near_slots = ring_gather(image, "x", core)
    text_near_slots = ring_gather(text, "z", core, image_near_slots[1])
    text_far_slots = ring_gather(text_far, "z", core)
    image_far_slots = ring_gather(image_far, "x", core)
    image_near_other = swap(jnp.concatenate(image_near_slots), "core")
    image_far_other = [swap(a, "core") for a in image_far_slots]

    back = jnp.arange(RING, dtype=jnp.int32)
    pair = jnp.arange(2, dtype=jnp.int32)
    x_of = (lax.axis_index("x") - back) % RING
    z_of = (lax.axis_index("z") - back) % RING
    yhi_of = lax.axis_index("yhi") ^ pair
    ylo_of = lax.axis_index("ylo") ^ pair
    core_of = core ^ pair
    image_ids = (((lax.axis_index("ylo") * 4 + lax.axis_index("z")) * 4 + x_of[None, None, :]) * 4
                 + yhi_of[:, None, None] * 2 + core_of[None, :, None]).reshape(2, 2 * RING) * rows
    text_ids = ((lax.axis_index("yhi") * 2 + core) * 32
                + (ylo_of[:, None] * 4 + z_of[None, :]) * 4 + lax.axis_index("x")).reshape(-1) * rows
    col_ids = (text_ids[:, None] + jnp.arange(rows, dtype=jnp.int32)).reshape(1, -1)

    same = image_ids[:, :, None] == text_ids
    pairs = jnp.max(jnp.where(same, jnp.arange(2 * RING, dtype=jnp.int32), -1), axis=2)

    scale = (inverse_temp * jnp.float32(math.log2(math.e))).reshape(1)
    s_near, x_near, row_stat, col_stat, t_all = score_call(
        image_near_slots + [image_near_other], text_near_slots + text_far_slots, scale, pairs[0], [], rows,
        "score_near")
    s_far, x_far, row_stat, col_stat = score_call(
        image_far_slots + image_far_other, [t_all], scale, pairs[1], [row_stat, col_stat], rows, "score_far")

    row_stat, col_stat = ring_merge_call(
        row_stat, [ring_shift(row_stat, "x", step) for step in (1, 2, 3)],
        col_stat, [ring_shift(col_stat, "z", step) for step in (1, 2, 3)])
    row_stat, col_lse, col_loss = pair_merge_call(row_stat, swap(row_stat, "yhi"), col_stat, swap(col_stat, "ylo"))
    row_lse, row_loss = core_merge_call(row_stat, swap(row_stat, "core"))
    row_loss, row_finish = ring_total(row_loss, "z")
    col_loss, col_finish = ring_total(col_loss, "x")

    w_far, far_own, far_part = image_call(
        s_far, row_lse, 2 * RING, col_lse, image_ids[1], col_ids, t_all, rows, "image_far")
    far_send = far_part.astype(jnp.float16)
    far_other = swap(far_send, "core").reshape(RING, rows, -1)
    far_own = far_own.reshape(RING, rows, -1)
    w_near, text_part = text_call(
        s_near, after(row_lse, far_send, row_loss, col_loss), 0, col_lse, image_ids[0], col_ids,
        x_near, w_far, x_far, rows, "text_all")
    text_part = text_part.reshape(2, RING, rows, -1)
    row_loss, col_loss = row_finish(row_loss), col_finish(col_loss)

    text_two = after(text_part[:, 2], row_loss, col_loss).astype(jnp.float16)
    text_through = ring_split(text_two, "z", -1)
    far_two = summed(far_own[2], far_other[2]).astype(jnp.float16)
    far_through = ring_split(far_two, "x", -1)
    near_own, near_part = near_call(after(w_near, far_two, text_two), t_all, "image_near")
    row_loss = row_loss + swap(row_loss, "ylo")
    col_loss = col_loss + swap(col_loss, "yhi")
    near_send = after(near_part, far_through, row_loss, col_loss).astype(jnp.float16)
    near_other = swap(near_send, "core").reshape(RING, rows, -1)
    near_own = near_own.reshape(RING, rows, -1)

    far_left, far_right = ring_outgoing(
        summed(far_own[1], far_other[1]), summed(far_own[3], far_other[3]), far_through, core)
    image_far_sum = ring_arrived(summed(far_own[0], far_other[0]), far_left, far_right, "x").astype(jnp.float16)
    text_left, text_right = ring_outgoing(text_part[1, 1], text_part[1, 3], text_through[1], core)
    text_far_sum = ring_arrived(text_part[1, 0], text_left, text_right, "z").astype(jnp.float16)
    near_through = ring_split(summed(near_own[2], near_other[2]).astype(jnp.float16), "x", -1)
    near_left, near_right = ring_outgoing(
        summed(near_own[1], near_other[1]), summed(near_own[3], near_other[3]), near_through, core)
    text_left, text_right = ring_outgoing(text_part[0, 1], text_part[0, 3], text_through[0], core)
    col_loss = col_loss + swap(col_loss, "core")
    image_grad = (ring_arrived(summed(near_own[0], near_other[0]), near_left, near_right, "x")
                  + swap(image_far_sum, "yhi").astype(jnp.float32))
    text_grad = (ring_arrived(text_part[0, 0], text_left, text_right, "z")
                 + swap(text_far_sum, "ylo").astype(jnp.float32))

    loss_value = jnp.sum(row_loss + col_loss) * jnp.float32(math.log(2.0)) / (2.0 * 128 * rows)
    return loss_value, inverse_temp * image_grad, inverse_temp * text_grad


def solution(mesh):
    fine = Mesh(mesh.devices.reshape(2, 4, 4, 2, 2), AXES)
    text_spec = P(("yhi", "core", "ylo", "z", "x"), None)
    return jax.shard_map(
        on_device, mesh=fine, in_specs=(P(AXES, None), text_spec, P()),
        out_specs=(P(), P(AXES, None), text_spec), check_vma=False
    )
```

```python
import math

import jax
import jax.numpy as jnp
from jax import lax
from jax.experimental import pallas as pl
from jax.experimental.pallas import tpu as pltpu
from jax.sharding import Mesh, PartitionSpec as P

AXES = ("ylo", "z", "x", "yhi", "core")
RING = 4
TILE_SLOTS = 2
EXTRA = 16
UNITS = (256.0, 1.0, 2.0 ** -8, 2.0 ** -16, 2.0 ** -24)
VMEM_LIMIT = 12 * 1024 * 1024


def f32(*shape):
    return jax.ShapeDtypeStruct(shape, jnp.float32)


def bf16(*shape):
    return jax.ShapeDtypeStruct(shape, jnp.bfloat16)


def vmem_call(kernel, out_shape, name, flops, transcendentals, scalars, *args):
    vmem = pl.BlockSpec(memory_space=pltpu.VMEM)
    nbytes = sum(a.size * a.dtype.itemsize for a in args)
    nbytes += sum(math.prod(o.shape) * o.dtype.itemsize for o in out_shape)
    return pl.pallas_call(
        kernel,
        in_specs=[pl.BlockSpec(memory_space=pltpu.SMEM)] * len(scalars) + [vmem] * len(args),
        out_specs=[vmem] * len(out_shape),
        out_shape=out_shape,
        compiler_params=pltpu.CompilerParams(vmem_limit_bytes=VMEM_LIMIT),
        cost_estimate=pl.CostEstimate(flops=flops, bytes_accessed=nbytes, transcendentals=transcendentals),
        name=name,
    )(*scalars, *args)


def to_lanes(column):
    return jnp.broadcast_to(column, (column.shape[0], 128)).T[0:1, :]


def to_rows(line):
    return jnp.broadcast_to(line, (128, line.shape[1])).T[:, 0:1]


def merge(stats):
    top = stats[0][0]
    for stat in stats[1:]:
        top = jnp.maximum(top, stat[0])
    total = sum(stat[1] * jnp.exp2(stat[0] - top) for stat in stats)
    return [top, total] + [sum(stat[k] for stat in stats) for k in range(2, len(stats[0]))]


def place_refs(refs):
    return {axis: refs[k][0] for k, axis in enumerate(AXES)}


def image_block(place, h, slot):
    x = lax.rem(place["x"] + RING - slot % RING, RING)
    core = place["core"] if slot < RING else 1 - place["core"]
    yhi = place["yhi"] if h == 0 else 1 - place["yhi"]
    return ((place["ylo"] * 4 + place["z"]) * 4 + x) * 4 + yhi * 2 + core


def text_block(place, slot):
    z = lax.rem(place["z"] + RING - slot % RING, RING)
    ylo = place["ylo"] if slot < RING else 1 - place["ylo"]
    return (place["yhi"] * 2 + place["core"]) * 32 + (ylo * 4 + z) * 4 + place["x"]


def score_call(images, texts, scale, place, h, near_stats, rows, name):
    width = images[0].shape[1]
    sizes = [a.shape[0] for a in images]
    text_sizes = [a.shape[0] for a in texts]
    m, n = sum(sizes), sum(text_sizes)
    slots = m // rows
    before = near_stats[0].shape[1] if near_stats else 0
    keep_text = len(texts) > 1

    def kernel(scale_ref, *refs):
        place, refs = place_refs(refs), refs[len(AXES):]
        image_refs, refs = refs[:len(images)], refs[len(images):]
        text_refs, refs = refs[:len(texts)], refs[len(texts):]
        held, refs = refs[:len(near_stats)], refs[len(near_stats):]
        s_ref, x_ref, row_ref, col_ref = refs[:4]
        t_ref = refs[4] if keep_text else text_refs[0]

        def fill(target, sources, counts):
            at = 0
            for source, count in zip(sources, counts):
                target[pl.ds(at, count), :] = source[...]
                at += count

        if keep_text:
            fill(t_ref, text_refs, text_sizes)
        fill(x_ref, image_refs, sizes)
        tile = rows * TILE_SLOTS
        tiles = m // tile
        scale = scale_ref[0]
        col_parts = []

        def scores(i):
            s_ref[pl.ds(i * tile, tile), :] = scale * lax.dot_general(
                x_ref[pl.ds(i * tile, tile), :], t_ref[...], (((1,), (1,)), ((), ())),
                preferred_element_type=jnp.float32)

        def stats(i):
            s = s_ref[pl.ds(i * tile, tile), :]
            col_top = jnp.max(s, axis=0, keepdims=True)
            col_parts.append((col_top, jnp.sum(jnp.exp2(s - col_top), axis=0, keepdims=True)))
            for j in range(TILE_SLOTS):
                slot = i * TILE_SLOTS + j
                s = s_ref[pl.ds(slot * rows, rows), :]
                row_top = jnp.max(s, axis=1, keepdims=True)
                row_sum = jnp.sum(jnp.exp2(s - row_top), axis=1, keepdims=True)
                row_ref[0, pl.ds(before + slot, 1), :] = to_lanes(row_top)
                row_ref[1, pl.ds(before + slot, 1), :] = to_lanes(row_sum)

        scores(0)
        for i in range(tiles):
            if i + 1 < tiles:
                scores(i + 1)
            stats(i)
        top, total = merge(col_parts)
        for k in range(n // rows):
            at = slice(k * rows, (k + 1) * rows)
            part = [(top[:, at], total[:, at])]
            if held:
                part.append((held[1][0, pl.ds(k, 1), :], held[1][1, pl.ds(k, 1), :]))
            col_ref[0, pl.ds(k, 1), :], col_ref[1, pl.ds(k, 1), :] = merge(part)
        if held:
            row_ref[:, pl.ds(0, before), :] = held[0][...]
        row_ref[2, pl.ds(before, slots), :] = jnp.zeros((slots, rows), jnp.float32)
        for slot in range(slots):
            for k in range(n // rows):
                @pl.when(image_block(place, h, slot) == text_block(place, k))
                def _():
                    s = s_ref[pl.ds(slot * rows, rows), :][:, k * rows:(k + 1) * rows]
                    mask = (lax.broadcasted_iota(jnp.int32, (rows, 1), 0)
                            == lax.broadcasted_iota(jnp.int32, (1, rows), 1))
                    row_ref[2, pl.ds(before + slot, 1), :] = jnp.sum(jnp.where(mask, s, 0.0), axis=0, keepdims=True)

    out_shape = [f32(m, n), bf16(m, width), f32(3, before + slots, rows), f32(2, n // rows, rows)]
    out_shape += [bf16(n, width)] * keep_text
    return vmem_call(kernel, out_shape, name, 2 * m * n * width, 2 * m * n, [scale, *place],
                     *images, *texts, *near_stats)


def turned(ref, k, step):
    rings = []
    for lo in range(0, ref.shape[1], RING):
        rings.append(ref[k, pl.ds(lo + RING - step, step), :])
        rings.append(ref[k, pl.ds(lo, RING - step), :])
    return jnp.concatenate(rings, axis=0)


def swapped(ref, k, group):
    parts = []
    for lo in range(0, ref.shape[1], 2 * group):
        parts.append(ref[k, pl.ds(lo + group, group), :])
        parts.append(ref[k, pl.ds(lo, group), :])
    return jnp.concatenate(parts, axis=0)


def ring_merge_call(row, rows_in, col, cols_in):
    def kernel(*refs):
        row_refs, col_refs = refs[:RING], refs[RING:2 * RING]
        for own, out in ((row_refs, refs[-2]), (col_refs, refs[-1])):
            planes = out.shape[0]
            stats = [[own[0][k] for k in range(planes)]]
            for step in range(1, RING):
                stats.append([turned(own[step], k, step) for k in range(planes)])
            for k, value in enumerate(merge(stats)):
                out[k] = value

    return vmem_call(kernel, [f32(*row.shape), f32(*col.shape)], "merge_ring", 0, 0, [],
                     row, *rows_in, col, *cols_in)


def pair_merge_call(row, row_in, col, col_in, loss_scale):
    half = col.shape[1] // 2

    def kernel(row_ref, row_in_ref, col_ref, col_in_ref, row_out, lse_ref, loss_ref):
        planes = range(row_ref.shape[0])
        for k, value in enumerate(merge([
                [row_ref[k] for k in planes], [swapped(row_in_ref, k, row_ref.shape[1] // 2) for k in planes]])):
            row_out[k] = value
        top, total = merge([[col_ref[k] for k in range(2)], [swapped(col_in_ref, k, half) for k in range(2)]])
        lse = top + jnp.log2(total)
        lse_ref[...] = lse
        loss_ref[...] = jnp.sum(lse, axis=0, keepdims=True) * loss_scale

    return vmem_call(kernel, [f32(*row.shape), f32(*col.shape[1:]), f32(1, col.shape[2])], "merge_pair", 0, 0, [],
                     row, row_in, col, col_in)


def core_merge_call(row, row_in, loss_scale):
    def kernel(row_ref, row_in_ref, lse_ref, loss_ref):
        planes = range(row_ref.shape[0])
        top, total, own = merge([[row_ref[k] for k in planes], [swapped(row_in_ref, k, RING) for k in planes]])
        lse = top + jnp.log2(total)
        lse_ref[...] = lse
        loss_ref[...] = jnp.sum(lse - 2.0 * own, axis=0, keepdims=True) * loss_scale

    return vmem_call(kernel, [f32(*row.shape[1:]), f32(1, row.shape[2])], "merge_core", 0, 0, [], row, row_in)


def soft_weights(v, row_lse, col_lse, first_id, col_ids):
    ids = first_id + lax.broadcasted_iota(jnp.int32, (v.shape[0], 1), 0)
    soft = 0.5 * (jnp.exp2(v - to_rows(row_lse)) + jnp.exp2(v - col_lse))
    return (soft - jnp.where(ids == col_ids, 1.0, 0.0)).astype(jnp.bfloat16)


def weight_steps(w_ref, s_ref, row_ref, col_ref, place, h, rows):
    slots = range(col_ref.shape[0])
    col_lse = jnp.concatenate([col_ref[pl.ds(k, 1), :] for k in slots], axis=1)
    within = lax.broadcasted_iota(jnp.int32, (1, rows), 1)
    col_ids = jnp.concatenate([text_block(place, k) * rows + within for k in slots], axis=1)
    first = h * 2 * RING

    def weights(i):
        for j in range(TILE_SLOTS):
            slot = i * TILE_SLOTS + j
            at = pl.ds(slot * rows, rows)
            w_ref[at, :] = soft_weights(
                s_ref[at, :], row_ref[pl.ds(first + slot, 1), :], col_lse, image_block(place, h, slot) * rows, col_ids)

    return weights


def put_digits(part_ref, loss_ref, rows):
    left = jnp.sum(loss_ref[...], axis=1, keepdims=True)
    number = lax.broadcasted_iota(jnp.int32, (EXTRA, 1), 0)
    block = jnp.zeros((EXTRA, 1), jnp.float32)
    for k, unit in enumerate(UNITS):
        digit = jnp.floor(left * (1.0 / unit) + 0.5)
        left = left - digit * unit
        block = jnp.where(number == k, digit, block)
    for slot in range(part_ref.shape[0]):
        part_ref[slot, pl.ds(rows, EXTRA), :] = jnp.broadcast_to(block, (EXTRA, part_ref.shape[2]))


def put_slots(own_ref, other_ref, slot, part, rows):
    for j in range(part.shape[0] // rows):
        out = own_ref if slot + j < RING else other_ref
        out[(slot + j) % RING, pl.ds(0, rows), :] = part[j * rows:(j + 1) * rows]


def image_call(s, row_lse, col_lse, loss, place, text, rows, name):
    m, n = s.shape
    width = text.shape[1]

    def kernel(*refs):
        place, refs = place_refs(refs), refs[len(AXES):]
        s_ref, row_ref, col_ref, loss_ref, t_ref, w_ref, own_ref, other_ref = refs
        tile = rows * TILE_SLOTS
        tiles = m // tile
        weights = weight_steps(w_ref, s_ref, row_ref, col_ref, place, 1, rows)
        put_digits(own_ref, loss_ref, rows)
        other_ref[:, pl.ds(rows, EXTRA), :] = own_ref[:, pl.ds(rows, EXTRA), :]

        def dots(i):
            put_slots(own_ref, other_ref, i * TILE_SLOTS, jnp.dot(
                w_ref[pl.ds(i * tile, tile), :], t_ref[...], preferred_element_type=jnp.float32), rows)

        weights(0)
        for i in range(tiles):
            if i + 1 < tiles:
                weights(i + 1)
            dots(i)

    parts = [f32(RING, rows + EXTRA, width)] * 2
    return vmem_call(kernel, [bf16(m, n)] + parts, name, 2 * m * n * width, 2 * m * n,
                     place, s, row_lse, col_lse, loss, text)


def text_call(s, row_lse, col_lse, loss, place, x_near, w_far, x_far, rows, name):
    m, n = s.shape
    width = x_near.shape[1]
    chunk = 384

    def kernel(*refs):
        place, refs = place_refs(refs), refs[len(AXES):]
        s_ref, row_ref, col_ref, loss_ref, xn_ref, wf_ref, xf_ref, w_ref, part_ref = refs
        tiles = m // (rows * TILE_SLOTS)
        dims = (((0,), (0,)), ((), ()))
        weights = weight_steps(w_ref, s_ref, row_ref, col_ref, place, 0, rows)
        put_digits(part_ref, loss_ref, rows)
        weights(0)
        for j in range(width // chunk):
            at = pl.ds(j * chunk, chunk)
            part = lax.dot_general(wf_ref[...], xf_ref[:, at], dims, preferred_element_type=jnp.float32)
            for k in range(n // rows):
                part_ref[k, pl.ds(0, rows), at] = part[k * rows:(k + 1) * rows]
            if j + 1 < tiles:
                weights(j + 1)
        for j in range(width // chunk):
            at = pl.ds(j * chunk, chunk)
            part = lax.dot_general(w_ref[...], xn_ref[:, at], dims, preferred_element_type=jnp.float32)
            for k in range(n // rows):
                part_ref[k, pl.ds(0, rows), at] += part[k * rows:(k + 1) * rows]

    return vmem_call(kernel, [bf16(m, n), f32(n // rows, rows + EXTRA, width)], name,
                     4 * m * n * width, 2 * m * n, place, s, row_lse, col_lse, loss, x_near, w_far, x_far)


def near_call(w, text, loss, rows, name):
    m, n = w.shape
    width = text.shape[1]
    half = m // 2

    def kernel(w_ref, t_ref, loss_ref, own_ref, other_ref):
        put_digits(own_ref, loss_ref, rows)
        other_ref[:, pl.ds(rows, EXTRA), :] = own_ref[:, pl.ds(rows, EXTRA), :]
        for slot in (RING, 0):
            put_slots(own_ref, other_ref, slot, jnp.dot(
                w_ref[pl.ds(slot * rows, half), :], t_ref[...], preferred_element_type=jnp.float32), rows)

    parts = [f32(RING, rows + EXTRA, width)] * 2
    return vmem_call(kernel, parts, name, 2 * m * n * width, 0, [], w, text, loss)


def after(value, *others):
    return lax.optimization_barrier((value, *others))[0]


def ring_shift(value, axis, step):
    return lax.ppermute(value, axis, [(i, (i + step) % RING) for i in range(RING)])


def ring_split(value, axis, sign):
    pairs = []
    for i in range(RING):
        for core in range(2):
            target = (i + (sign if core == 0 else -sign)) % RING
            pairs.append((i * 2 + core, target * 2 + core))
    return lax.ppermute(value, (axis, "core"), pairs)


def swap(value, axis):
    return lax.ppermute(value, axis, [(0, 1), (1, 0)])


def ring_gather(value, axis, core):
    one = ring_shift(value, axis, 1)
    three = ring_shift(value, axis, 3)
    two = ring_split(jnp.where(core == 0, one, three), axis, 1)
    return [value, one, two, three]


def summed(own, other):
    return own + other.astype(jnp.float32)


def ring_outgoing(one, three, through, core):
    through = through.astype(jnp.float32)
    left = one + jnp.where(core == 0, through, 0.0)
    right = three + jnp.where(core == 0, 0.0, through)
    return left.astype(jnp.float16), right.astype(jnp.float16)


def ring_arrived(own, left, right, axis):
    return own + ring_shift(left, axis, -1).astype(jnp.float32) + ring_shift(right, axis, 1).astype(jnp.float32)


def on_device(image, text, log_scale):
    inverse_temp = jnp.exp(log_scale)
    rows = image.shape[0]
    core = lax.axis_index("core")
    place = [lax.axis_index(axis).reshape(1) for axis in AXES]

    text_far = swap(text, "ylo")
    image = after(image, text_far)
    image_far = swap(image, "yhi")
    text_near_slots = ring_gather(text, "z", core)
    text_far_slots = ring_gather(text_far, "z", core)
    image_near_slots = ring_gather(image, "x", core)
    image_far_slots = ring_gather(image_far, "x", core)
    image_near_other = swap(jnp.concatenate(image_near_slots), "core")
    image_far_other = [swap(a, "core") for a in image_far_slots]

    scale = (inverse_temp * jnp.float32(math.log2(math.e))).reshape(1)
    s_near, x_near, row_stat, col_stat, t_all = score_call(
        image_near_slots + [image_near_other], text_near_slots + text_far_slots, scale, place, 0, [], rows,
        "score_near")
    s_far, x_far, row_stat, col_stat = score_call(
        image_far_slots + image_far_other, [t_all], scale, place, 1, [row_stat, col_stat], rows, "score_far")

    loss_scale = math.log(2.0) / (2 * 128 * rows)
    row_stat, col_stat = ring_merge_call(
        row_stat, [ring_shift(row_stat, "x", step) for step in (1, 2, 3)],
        col_stat, [ring_shift(col_stat, "z", step) for step in (1, 2, 3)])
    row_stat, col_lse, col_loss = pair_merge_call(
        row_stat, swap(row_stat, "yhi"), col_stat, swap(col_stat, "ylo"), loss_scale)
    row_lse, row_loss = core_merge_call(row_stat, swap(row_stat, "core"), loss_scale)

    w_far, far_own, far_part = image_call(s_far, row_lse, col_lse, col_loss, place, t_all, rows, "image_far")
    far_send = far_part.astype(jnp.float16)
    far_other = swap(far_send, "core")
    w_near, text_part = text_call(
        s_near, after(row_lse, far_send), col_lse, row_loss, place, x_near, w_far, x_far, rows, "text_all")
    near_text, far_text = text_part[:RING], text_part[RING:]
    text_two = jnp.stack([near_text[2], far_text[2]]).astype(jnp.float16)
    text_through = ring_split(text_two, "z", -1)
    far_two = summed(far_own[2], after(far_other, text_two)[2]).astype(jnp.float16)
    far_through = ring_split(far_two, "x", -1)
    near_own, near_part = near_call(after(w_near, far_two), t_all, col_loss, rows, "image_near")
    near_send = near_part.astype(jnp.float16)
    near_other = swap(near_send, "core")

    far_left, far_right = ring_outgoing(
        summed(far_own[1], far_other[1]), summed(far_own[3], far_other[3]), after(far_through, near_send), core)
    far_text_left, far_text_right = ring_outgoing(
        far_text[1], far_text[3], after(text_through, far_left)[1], core)
    near_two = summed(near_own[2], after(near_other, far_text_left)[2]).astype(jnp.float16)
    near_through = ring_split(near_two, "x", -1)
    near_text_left, near_text_right = ring_outgoing(
        near_text[1], near_text[3], after(text_through, near_two)[0], core)
    image_far_sum = ring_arrived(
        summed(far_own[0], after(far_other, near_text_left)[0]), far_left, far_right, "x").astype(jnp.float16)
    text_far_sum = ring_arrived(
        after(far_text[0], image_far_sum), far_text_left, far_text_right, "z").astype(jnp.float16)
    near_left, near_right = ring_outgoing(
        summed(near_own[1], near_other[1]), summed(near_own[3], near_other[3]), after(near_through, text_far_sum), core)
    text_sum = (ring_arrived(after(near_text[0], near_left), near_text_left, near_text_right, "z")
                + swap(text_far_sum, "ylo").astype(jnp.float32))
    image_sum = (ring_arrived(summed(near_own[0], near_other[0]), near_left, near_right, "x")
                 + swap(image_far_sum, "yhi").astype(jnp.float32))

    digits = text_sum[rows:, 0] + image_sum[rows:, 0]
    loss_value = sum(digits[k] * unit for k, unit in enumerate(UNITS))
    return loss_value, inverse_temp * image_sum[:rows], inverse_temp * text_sum[:rows]


def solution(mesh):
    fine = Mesh(mesh.devices.reshape(2, 4, 4, 2, 2), AXES)
    text_spec = P(("yhi", "core", "ylo", "z", "x"), None)
    return jax.shard_map(
        on_device, mesh=fine, in_specs=(P(AXES, None), text_spec, P()),
        out_specs=(P(), P(AXES, None), text_spec), check_vma=False
    )
```

```python
import functools
import math

import jax
import jax.numpy as jnp
from jax import lax
from jax.experimental import pallas as pl
from jax.experimental.pallas import tpu as pltpu
from jax.sharding import Mesh, PartitionSpec as P

AXES = ("ylo", "z", "x", "yhi", "core")
RING = 4
TILE_SLOTS = 2
EXTRA = 16
UNITS = (256.0, 1.0, 2.0 ** -8, 2.0 ** -16, 2.0 ** -24)
VMEM_LIMIT = 12 * 1024 * 1024


def f32(*shape):
    return jax.ShapeDtypeStruct(shape, jnp.float32)


def bf16(*shape):
    return jax.ShapeDtypeStruct(shape, jnp.bfloat16)


def vmem_call(kernel, out_shape, name, flops, transcendentals, scalars, *args):
    vmem = pl.BlockSpec(memory_space=pltpu.VMEM)
    nbytes = sum(a.size * a.dtype.itemsize for a in args)
    nbytes += sum(math.prod(o.shape) * o.dtype.itemsize for o in out_shape)
    return pl.pallas_call(
        kernel,
        in_specs=[pl.BlockSpec(memory_space=pltpu.SMEM)] * len(scalars) + [vmem] * len(args),
        out_specs=[vmem] * len(out_shape),
        out_shape=out_shape,
        compiler_params=pltpu.CompilerParams(vmem_limit_bytes=VMEM_LIMIT),
        cost_estimate=pl.CostEstimate(flops=flops, bytes_accessed=nbytes, transcendentals=transcendentals),
        name=name,
    )(*scalars, *args)


def to_lanes(column):
    return jnp.broadcast_to(column, (column.shape[0], 128)).T[0:1, :]


def to_rows(line):
    return jnp.broadcast_to(line, (128, line.shape[1])).T[:, 0:1]


def merge(stats):
    top = stats[0][0]
    for stat in stats[1:]:
        top = jnp.maximum(top, stat[0])
    total = sum(stat[1] * jnp.exp2(stat[0] - top) for stat in stats)
    return [top, total] + [sum(stat[k] for stat in stats) for k in range(2, len(stats[0]))]


def place_refs(refs):
    return {axis: refs[k][0] for k, axis in enumerate(AXES)}


def image_block(place, h, slot):
    x = lax.rem(place["x"] + RING - slot % RING, RING)
    core = place["core"] if slot < RING else 1 - place["core"]
    yhi = place["yhi"] if h == 0 else 1 - place["yhi"]
    return ((place["ylo"] * 4 + place["z"]) * 4 + x) * 4 + yhi * 2 + core


def text_block(place, slot):
    z = lax.rem(place["z"] + RING - slot % RING, RING)
    ylo = place["ylo"] if slot < RING else 1 - place["ylo"]
    return (place["yhi"] * 2 + place["core"]) * 32 + (ylo * 4 + z) * 4 + place["x"]


def score_call(images, texts, scale, place, h, near_stats, rows, name):
    width = images[0].shape[1]
    sizes = [a.shape[0] for a in images]
    text_sizes = [a.shape[0] for a in texts]
    m, n = sum(sizes), sum(text_sizes)
    slots = m // rows
    before = near_stats[0].shape[1] if near_stats else 0
    keep_text = len(texts) > 1

    def kernel(scale_ref, *refs):
        place, refs = place_refs(refs), refs[len(AXES):]
        image_refs, refs = refs[:len(images)], refs[len(images):]
        text_refs, refs = refs[:len(texts)], refs[len(texts):]
        held, refs = refs[:len(near_stats)], refs[len(near_stats):]
        s_ref, x_ref, row_ref, col_ref = refs[:4]
        t_ref = refs[4] if keep_text else text_refs[0]

        def fill(target, sources, counts):
            at = 0
            for source, count in zip(sources, counts):
                target[pl.ds(at, count), :] = source[...]
                at += count

        if keep_text:
            fill(t_ref, text_refs, text_sizes)
        fill(x_ref, image_refs, sizes)
        tile = rows * TILE_SLOTS
        tiles = m // tile
        scale = scale_ref[0]
        col_parts = []

        def scores(i):
            s_ref[pl.ds(i * tile, tile), :] = scale * lax.dot_general(
                x_ref[pl.ds(i * tile, tile), :], t_ref[...], (((1,), (1,)), ((), ())),
                preferred_element_type=jnp.float32)

        def stats(i):
            s = s_ref[pl.ds(i * tile, tile), :]
            col_top = jnp.max(s, axis=0, keepdims=True)
            col_parts.append((col_top, jnp.sum(jnp.exp2(s - col_top), axis=0, keepdims=True)))
            for j in range(TILE_SLOTS):
                slot = i * TILE_SLOTS + j
                s = s_ref[pl.ds(slot * rows, rows), :]
                row_top = jnp.max(s, axis=1, keepdims=True)
                row_sum = jnp.sum(jnp.exp2(s - row_top), axis=1, keepdims=True)
                row_ref[0, pl.ds(before + slot, 1), :] = to_lanes(row_top)
                row_ref[1, pl.ds(before + slot, 1), :] = to_lanes(row_sum)

        scores(0)
        for i in range(tiles):
            if i + 1 < tiles:
                scores(i + 1)
            stats(i)
        top, total = merge(col_parts)
        for k in range(n // rows):
            at = slice(k * rows, (k + 1) * rows)
            part = [(top[:, at], total[:, at])]
            if held:
                part.append((held[1][0, pl.ds(k, 1), :], held[1][1, pl.ds(k, 1), :]))
            col_ref[0, pl.ds(k, 1), :], col_ref[1, pl.ds(k, 1), :] = merge(part)
        if held:
            row_ref[:, pl.ds(0, before), :] = held[0][...]
        row_ref[2, pl.ds(before, slots), :] = jnp.zeros((slots, rows), jnp.float32)
        for slot in range(slots):
            for k in range(n // rows):
                @pl.when(image_block(place, h, slot) == text_block(place, k))
                def _():
                    s = s_ref[pl.ds(slot * rows, rows), :][:, k * rows:(k + 1) * rows]
                    mask = (lax.broadcasted_iota(jnp.int32, (rows, 1), 0)
                            == lax.broadcasted_iota(jnp.int32, (1, rows), 1))
                    row_ref[2, pl.ds(before + slot, 1), :] = jnp.sum(jnp.where(mask, s, 0.0), axis=0, keepdims=True)

    out_shape = [f32(m, n), bf16(m, width), f32(3, before + slots, rows), f32(2, n // rows, rows)]
    out_shape += [bf16(n, width)] * keep_text
    return vmem_call(kernel, out_shape, name, 2 * m * n * width, 2 * m * n, [scale, *place],
                     *images, *texts, *near_stats)


def turned(ref, k, step):
    rings = []
    for lo in range(0, ref.shape[1], RING):
        rings.append(ref[k, pl.ds(lo + RING - step, step), :])
        rings.append(ref[k, pl.ds(lo, RING - step), :])
    return jnp.concatenate(rings, axis=0)


def swapped(ref, k, group):
    parts = []
    for lo in range(0, ref.shape[1], 2 * group):
        parts.append(ref[k, pl.ds(lo + group, group), :])
        parts.append(ref[k, pl.ds(lo, group), :])
    return jnp.concatenate(parts, axis=0)


def merge_call(row, row_in, row_order, col, col_in, col_order, loss_scale, name):
    arrays = [row, row_in] + ([] if col is None else [col, col_in])
    pairs = [(row, row_order, 0)] + ([] if col is None else [(col, col_order, 2)])
    out_shape = []
    for stat, _, k in pairs:
        done = loss_scale[k // 2] is not None
        out_shape += [f32(*stat.shape[1:]), f32(1, stat.shape[2])] if done else [f32(*stat.shape)]

    def kernel(*refs):
        outs = list(refs[len(arrays):])
        for stat, order, k in pairs:
            planes = range(stat.shape[0])
            merged = merge([[refs[k][p] for p in planes], [order(refs[k + 1], p) for p in planes]])
            if loss_scale[k // 2] is None:
                out = outs.pop(0)
                for p in planes:
                    out[p] = merged[p]
            else:
                lse = merged[0] + jnp.log2(merged[1])
                outs.pop(0)[...] = lse
                own = 2.0 * merged[2] if len(merged) > 2 else 0.0
                outs.pop(0)[...] = jnp.sum(lse - own, axis=0, keepdims=True) * loss_scale[k // 2]

    return vmem_call(kernel, out_shape, name, 0, 0, [], *arrays)


def join_call(parts, name):
    def kernel(*refs):
        at = 0
        for ref in refs[:-1]:
            refs[-1][pl.ds(at, ref.shape[0]), :] = ref[...]
            at += ref.shape[0]

    return vmem_call(kernel, [bf16(sum(p.shape[0] for p in parts), parts[0].shape[1])], name, 0, 0, [], *parts)[0]


def soft_weights(v, row_lse, col_lse, first_id, col_ids):
    ids = first_id + lax.broadcasted_iota(jnp.int32, (v.shape[0], 1), 0)
    soft = 0.5 * (jnp.exp2(v - to_rows(row_lse)) + jnp.exp2(v - col_lse))
    return (soft - jnp.where(ids == col_ids, 1.0, 0.0)).astype(jnp.bfloat16)


def weight_steps(w_ref, s_ref, row_ref, col_ref, place, h, rows):
    slots = range(col_ref.shape[0])
    col_lse = jnp.concatenate([col_ref[pl.ds(k, 1), :] for k in slots], axis=1)
    within = lax.broadcasted_iota(jnp.int32, (1, rows), 1)
    col_ids = jnp.concatenate([text_block(place, k) * rows + within for k in slots], axis=1)
    first = h * 2 * RING

    def weights(i):
        for j in range(TILE_SLOTS):
            slot = i * TILE_SLOTS + j
            at = pl.ds(slot * rows, rows)
            w_ref[at, :] = soft_weights(
                s_ref[at, :], row_ref[pl.ds(first + slot, 1), :], col_lse, image_block(place, h, slot) * rows, col_ids)

    return weights


def put_digits(part_ref, loss_ref, rows):
    left = jnp.sum(loss_ref[...], axis=1, keepdims=True)
    number = lax.broadcasted_iota(jnp.int32, (EXTRA, 1), 0)
    block = jnp.zeros((EXTRA, 1), jnp.float32)
    for k, unit in enumerate(UNITS):
        digit = jnp.floor(left * (1.0 / unit) + 0.5)
        left = left - digit * unit
        block = jnp.where(number == k, digit, block)
    for slot in range(part_ref.shape[0]):
        part_ref[slot, pl.ds(rows, EXTRA), :] = jnp.broadcast_to(block, (EXTRA, part_ref.shape[2]))


def put_slots(own_ref, other_ref, slot, part, rows):
    for j in range(part.shape[0] // rows):
        out = own_ref if slot + j < RING else other_ref
        out[(slot + j) % RING, pl.ds(0, rows), :] = part[j * rows:(j + 1) * rows]


def image_call(s, row_lse, col_lse, loss, place, text, rows, name):
    m, n = s.shape
    width = text.shape[1]

    def kernel(*refs):
        place, refs = place_refs(refs), refs[len(AXES):]
        s_ref, row_ref, col_ref, loss_ref, t_ref, w_ref, own_ref, other_ref = refs
        tile = rows * TILE_SLOTS
        tiles = m // tile
        weights = weight_steps(w_ref, s_ref, row_ref, col_ref, place, 1, rows)
        put_digits(own_ref, loss_ref, rows)
        other_ref[:, pl.ds(rows, EXTRA), :] = own_ref[:, pl.ds(rows, EXTRA), :]

        def dots(i):
            put_slots(own_ref, other_ref, i * TILE_SLOTS, jnp.dot(
                w_ref[pl.ds(i * tile, tile), :], t_ref[...], preferred_element_type=jnp.float32), rows)

        weights(0)
        for i in range(tiles):
            if i + 1 < tiles:
                weights(i + 1)
            dots(i)

    parts = [f32(RING, rows + EXTRA, width)] * 2
    return vmem_call(kernel, [bf16(m, n)] + parts, name, 2 * m * n * width, 2 * m * n,
                     place, s, row_lse, col_lse, loss, text)


def text_call(s, row_lse, col_lse, loss, place, x_near, w_far, x_far, rows, name):
    m, n = s.shape
    width = x_near.shape[1]
    chunk = 384

    def kernel(*refs):
        place, refs = place_refs(refs), refs[len(AXES):]
        s_ref, row_ref, col_ref, loss_ref, xn_ref, wf_ref, xf_ref, w_ref, part_ref = refs
        tiles = m // (rows * TILE_SLOTS)
        dims = (((0,), (0,)), ((), ()))
        weights = weight_steps(w_ref, s_ref, row_ref, col_ref, place, 0, rows)
        put_digits(part_ref, loss_ref, rows)
        weights(0)
        for j in range(width // chunk):
            at = pl.ds(j * chunk, chunk)
            part = lax.dot_general(wf_ref[...], xf_ref[:, at], dims, preferred_element_type=jnp.float32)
            for k in range(n // rows):
                part_ref[k, pl.ds(0, rows), at] = part[k * rows:(k + 1) * rows]
            if j + 1 < tiles:
                weights(j + 1)
        for j in range(width // chunk):
            at = pl.ds(j * chunk, chunk)
            part = lax.dot_general(w_ref[...], xn_ref[:, at], dims, preferred_element_type=jnp.float32)
            for k in range(n // rows):
                part_ref[k, pl.ds(0, rows), at] += part[k * rows:(k + 1) * rows]

    return vmem_call(kernel, [bf16(m, n), f32(n // rows, rows + EXTRA, width)], name,
                     4 * m * n * width, 2 * m * n, place, s, row_lse, col_lse, loss, x_near, w_far, x_far)


def near_call(w, text, loss, rows, name):
    m, n = w.shape
    width = text.shape[1]
    half = m // 2

    def kernel(w_ref, t_ref, loss_ref, own_ref, other_ref):
        put_digits(own_ref, loss_ref, rows)
        other_ref[:, pl.ds(rows, EXTRA), :] = own_ref[:, pl.ds(rows, EXTRA), :]
        for slot in (RING, 0):
            put_slots(own_ref, other_ref, slot, jnp.dot(
                w_ref[pl.ds(slot * rows, half), :], t_ref[...], preferred_element_type=jnp.float32), rows)

    parts = [f32(RING, rows + EXTRA, width)] * 2
    return vmem_call(kernel, parts, name, 2 * m * n * width, 0, [], w, text, loss)


def after(value, *others):
    return lax.optimization_barrier((value, *others))[0]


def ring_shift(value, axis, step):
    return lax.ppermute(value, axis, [(i, (i + step) % RING) for i in range(RING)])


def ring_split(value, axis, sign):
    pairs = []
    for i in range(RING):
        for core in range(2):
            target = (i + (sign if core == 0 else -sign)) % RING
            pairs.append((i * 2 + core, target * 2 + core))
    return lax.ppermute(value, (axis, "core"), pairs)


def swap(value, axis):
    return lax.ppermute(value, axis, [(0, 1), (1, 0)])


def ring_gather(value, axis, first_core, wait_for=None):
    one = ring_shift(value, axis, 1)
    three = ring_shift(value, axis, 3)
    two = ring_split(jnp.where(first_core, one, three if wait_for is None else after(three, wait_for)), axis, 1)
    return [value, one, two, three]


def summed(own, other):
    return own + other.astype(jnp.float32)


def ring_outgoing(one, three, through, first_core):
    through = through.astype(jnp.float32)
    left = one + jnp.where(first_core, through, 0.0)
    right = three + jnp.where(first_core, 0.0, through)
    return left.astype(jnp.float16), right.astype(jnp.float16)


def ring_arrived(own, left, right, axis):
    return own + ring_shift(left, axis, -1).astype(jnp.float32) + ring_shift(right, axis, 1).astype(jnp.float32)


def on_device(image, text, log_scale):
    inverse_temp = jnp.exp(log_scale)
    rows = image.shape[0]
    core = lax.axis_index("core")
    place = [lax.axis_index(axis).reshape(1) for axis in AXES]
    scale = (inverse_temp * jnp.float32(math.log2(math.e))).reshape(1)
    image, text, scale, place, first_core = lax.optimization_barrier((image, text, scale, place, core == 0))

    text_far = swap(text, "ylo")
    image_far = swap(image, "yhi")
    text_near_slots = ring_gather(text, "z", first_core)
    text_near = join_call(text_near_slots, "join_text")
    text_far_slots = ring_gather(text_far, "z", first_core, text_near)
    image_near_slots = ring_gather(image, "x", first_core)
    image_far_slots = ring_gather(image_far, "x", first_core)
    image_near = join_call(image_near_slots, "join_image")
    image_near_other = swap(image_near, "core")
    image_far_other = [swap(a, "core") for a in image_far_slots]

    s_near, x_near, row_stat, col_stat, t_all = score_call(
        [image_near, image_near_other], [text_near] + text_far_slots, scale, place, 0, [], rows, "score_near")
    s_far, x_far, row_stat, col_stat = score_call(
        image_far_slots + image_far_other, [t_all], scale, place, 1, [row_stat, col_stat], rows, "score_far")

    loss_scale = math.log(2.0) / (2 * 128 * rows)
    one, two = (functools.partial(turned, step=step) for step in (1, 2))
    cores, pairs = functools.partial(swapped, group=RING), functools.partial(swapped, group=2 * RING)
    row_stat, col_stat = merge_call(
        row_stat, swap(row_stat, "core"), cores, col_stat, ring_shift(col_stat, "z", 1), one,
        (None, None), "merge_core")
    row_stat, col_stat = merge_call(
        row_stat, ring_shift(row_stat, "x", 1), one, col_stat, ring_shift(col_stat, "z", 2), two,
        (None, None), "merge_one")
    row_stat, col_lse, col_loss = merge_call(
        row_stat, ring_shift(row_stat, "x", 2), two, col_stat, swap(col_stat, "ylo"), cores,
        (None, loss_scale), "merge_two")
    row_lse, row_loss = merge_call(
        row_stat, swap(row_stat, "yhi"), pairs, None, None, None, (loss_scale,), "merge_pair")

    w_far, far_own, far_part = image_call(s_far, row_lse, col_lse, col_loss, place, t_all, rows, "image_far")
    far_send = far_part.astype(jnp.float16)
    far_other = swap(far_send, "core")
    w_near, text_part = text_call(
        s_near, after(row_lse, far_send), col_lse, row_loss, place, x_near, w_far, x_far, rows, "text_all")
    near_text, far_text = text_part[:RING], text_part[RING:]
    text_two = jnp.stack([near_text[2], far_text[2]]).astype(jnp.float16)
    text_through = ring_split(text_two, "z", -1)
    far_two = summed(far_own[2], after(far_other, text_two)[2]).astype(jnp.float16)
    far_through = ring_split(far_two, "x", -1)
    near_own, near_part = near_call(after(w_near, far_two), t_all, col_loss, rows, "image_near")
    near_send = near_part.astype(jnp.float16)

    through, _, through_two = lax.optimization_barrier((far_through, near_send, text_through))
    far_left, far_right = ring_outgoing(
        summed(far_own[1], far_other[1]), summed(far_own[3], far_other[3]), through, first_core)
    near_other = swap(after(near_send, far_left), "core")
    text_left, text_right = ring_outgoing(
        far_text[1], far_text[3], after(through_two, far_left)[1], first_core)
    near_two = summed(near_own[2], after(near_other, text_left)[2]).astype(jnp.float16)
    near_through = ring_split(near_two, "x", -1)
    image_far_sum = ring_arrived(
        summed(far_own[0], after(far_other, near_two)[0]), far_left, far_right, "x").astype(jnp.float16)
    image_far_in = swap(image_far_sum, "yhi")
    near_left, near_right = ring_outgoing(
        summed(near_own[1], near_other[1]), summed(near_own[3], near_other[3]),
        after(near_through, image_far_sum), first_core)
    text_far_sum = ring_arrived(after(far_text[0], near_left), text_left, text_right, "z").astype(jnp.float16)
    near_text_left, near_text_right = ring_outgoing(
        near_text[1], near_text[3], after(through_two, image_far_sum)[0], first_core)
    image_sum = (ring_arrived(summed(near_own[0], near_other[0]), near_left, near_right, "x")
                 + image_far_in.astype(jnp.float32))
    text_sum = ring_arrived(near_text[0], near_text_left, near_text_right, "z") + swap(text_far_sum, "ylo").astype(jnp.float32)

    digits = text_sum[rows:, 0] + image_sum[rows:, 0]
    loss_value = sum(digits[k] * unit for k, unit in enumerate(UNITS))
    return loss_value, inverse_temp * image_sum[:rows], inverse_temp * text_sum[:rows]


def solution(mesh):
    fine = Mesh(mesh.devices.reshape(2, 4, 4, 2, 2), AXES)
    text_spec = P(("yhi", "core", "ylo", "z", "x"), None)
    return jax.shard_map(
        on_device, mesh=fine, in_specs=(P(AXES, None), text_spec, P()),
        out_specs=(P(), P(AXES, None), text_spec), check_vma=False
    )
```

```python
import functools
import math

import jax
import jax.numpy as jnp
from jax import lax
from jax.experimental import pallas as pl
from jax.experimental.pallas import tpu as pltpu
from jax.sharding import Mesh, PartitionSpec as P

AXES = ("ylo", "z", "x", "yhi", "core")
RING = 4
TILE_SLOTS = 2
EXTRA = 16
UNITS = (256.0, 1.0, 2.0 ** -8, 2.0 ** -16, 2.0 ** -24)
VMEM_LIMIT = 12 * 1024 * 1024


def f32(*shape):
    return jax.ShapeDtypeStruct(shape, jnp.float32)


def bf16(*shape):
    return jax.ShapeDtypeStruct(shape, jnp.bfloat16)


def vmem_call(kernel, out_shape, name, flops, transcendentals, scalars, *args):
    vmem = pl.BlockSpec(memory_space=pltpu.VMEM)
    nbytes = sum(a.size * a.dtype.itemsize for a in args)
    nbytes += sum(math.prod(o.shape) * o.dtype.itemsize for o in out_shape)
    return pl.pallas_call(
        kernel,
        in_specs=[pl.BlockSpec(memory_space=pltpu.SMEM)] * len(scalars) + [vmem] * len(args),
        out_specs=[vmem] * len(out_shape),
        out_shape=out_shape,
        compiler_params=pltpu.CompilerParams(vmem_limit_bytes=VMEM_LIMIT),
        cost_estimate=pl.CostEstimate(flops=flops, bytes_accessed=nbytes, transcendentals=transcendentals),
        name=name,
    )(*scalars, *args)


def to_lanes(column):
    return jnp.broadcast_to(column, (column.shape[0], 128)).T[0:1, :]


def to_rows(line):
    return jnp.broadcast_to(line, (128, line.shape[1])).T[:, 0:1]


def merge(stats):
    top = stats[0][0]
    for stat in stats[1:]:
        top = jnp.maximum(top, stat[0])
    total = sum(stat[1] * jnp.exp2(stat[0] - top) for stat in stats)
    return [top, total] + [sum(stat[k] for stat in stats) for k in range(2, len(stats[0]))]


def place_refs(refs):
    return {axis: refs[k][0] for k, axis in enumerate(AXES)}


def image_block(place, h, slot):
    x = lax.rem(place["x"] + RING - slot % RING, RING)
    core = place["core"] if slot < RING else 1 - place["core"]
    yhi = place["yhi"] if h == 0 else 1 - place["yhi"]
    return ((place["ylo"] * 4 + place["z"]) * 4 + x) * 4 + yhi * 2 + core


def text_block(place, slot):
    z = lax.rem(place["z"] + RING - slot % RING, RING)
    ylo = place["ylo"] if slot < RING else 1 - place["ylo"]
    return (place["yhi"] * 2 + place["core"]) * 32 + (ylo * 4 + z) * 4 + place["x"]


def score_call(images, texts, scale, place, h, near_stats, rows, name):
    width = images[0].shape[1]
    sizes = [a.shape[0] for a in images]
    text_sizes = [a.shape[0] for a in texts]
    m, n = sum(sizes), sum(text_sizes)
    slots = m // rows
    before = near_stats[0].shape[1] if near_stats else 0
    keep_text = len(texts) > 1

    def kernel(scale_ref, *refs):
        place, refs = place_refs(refs), refs[len(AXES):]
        image_refs, refs = refs[:len(images)], refs[len(images):]
        text_refs, refs = refs[:len(texts)], refs[len(texts):]
        held, refs = refs[:len(near_stats)], refs[len(near_stats):]
        s_ref, x_ref, row_ref, col_ref = refs[:4]
        t_ref = refs[4] if keep_text else text_refs[0]

        def fill(target, sources, counts):
            at = 0
            for source, count in zip(sources, counts):
                target[pl.ds(at, count), :] = source[...]
                at += count

        if keep_text:
            fill(t_ref, text_refs, text_sizes)
        fill(x_ref, image_refs, sizes)
        tile = rows * TILE_SLOTS
        tiles = m // tile
        scale = scale_ref[0]
        col_parts = []

        def scores(i):
            s_ref[pl.ds(i * tile, tile), :] = scale * lax.dot_general(
                x_ref[pl.ds(i * tile, tile), :], t_ref[...], (((1,), (1,)), ((), ())),
                preferred_element_type=jnp.float32)

        def stats(i):
            s = s_ref[pl.ds(i * tile, tile), :]
            col_top = jnp.max(s, axis=0, keepdims=True)
            col_parts.append((col_top, jnp.sum(jnp.exp2(s - col_top), axis=0, keepdims=True)))
            for j in range(TILE_SLOTS):
                slot = i * TILE_SLOTS + j
                s = s_ref[pl.ds(slot * rows, rows), :]
                row_top = jnp.max(s, axis=1, keepdims=True)
                row_sum = jnp.sum(jnp.exp2(s - row_top), axis=1, keepdims=True)
                row_ref[0, pl.ds(before + slot, 1), :] = to_lanes(row_top)
                row_ref[1, pl.ds(before + slot, 1), :] = to_lanes(row_sum)

        scores(0)
        for i in range(tiles):
            if i + 1 < tiles:
                scores(i + 1)
            stats(i)
        top, total = merge(col_parts)
        for k in range(n // rows):
            at = slice(k * rows, (k + 1) * rows)
            part = [(top[:, at], total[:, at])]
            if held:
                part.append((held[1][0, pl.ds(k, 1), :], held[1][1, pl.ds(k, 1), :]))
            col_ref[0, pl.ds(k, 1), :], col_ref[1, pl.ds(k, 1), :] = merge(part)
        if held:
            row_ref[:, pl.ds(0, before), :] = held[0][...]
        row_ref[2, pl.ds(before, slots), :] = jnp.zeros((slots, rows), jnp.float32)
        for slot in range(slots):
            for k in range(n // rows):
                @pl.when(image_block(place, h, slot) == text_block(place, k))
                def _():
                    s = s_ref[pl.ds(slot * rows, rows), :][:, k * rows:(k + 1) * rows]
                    mask = (lax.broadcasted_iota(jnp.int32, (rows, 1), 0)
                            == lax.broadcasted_iota(jnp.int32, (1, rows), 1))
                    row_ref[2, pl.ds(before + slot, 1), :] = jnp.sum(jnp.where(mask, s, 0.0), axis=0, keepdims=True)

    out_shape = [f32(m, n), bf16(m, width), f32(3, before + slots, rows), f32(2, n // rows, rows)]
    out_shape += [bf16(n, width)] * keep_text
    return vmem_call(kernel, out_shape, name, 2 * m * n * width, 2 * m * n, [scale, *place],
                     *images, *texts, *near_stats)


def turned(ref, k, step):
    rings = []
    for lo in range(0, ref.shape[1], RING):
        rings.append(ref[k, pl.ds(lo + RING - step, step), :])
        rings.append(ref[k, pl.ds(lo, RING - step), :])
    return jnp.concatenate(rings, axis=0)


def swapped(ref, k, group):
    parts = []
    for lo in range(0, ref.shape[1], 2 * group):
        parts.append(ref[k, pl.ds(lo + group, group), :])
        parts.append(ref[k, pl.ds(lo, group), :])
    return jnp.concatenate(parts, axis=0)


def merge_call(row, row_in, row_order, col, col_in, col_order, loss_scale, name):
    arrays = [row, row_in] + ([] if col is None else [col, col_in])
    pairs = [(row, row_order, 0)] + ([] if col is None else [(col, col_order, 2)])
    out_shape = []
    for stat, _, k in pairs:
        done = loss_scale[k // 2] is not None
        out_shape += [f32(*stat.shape[1:]), f32(1, stat.shape[2])] if done else [f32(*stat.shape)]

    def kernel(*refs):
        outs = list(refs[len(arrays):])
        for stat, order, k in pairs:
            planes = range(stat.shape[0])
            merged = merge([[refs[k][p] for p in planes], [order(refs[k + 1], p) for p in planes]])
            if loss_scale[k // 2] is None:
                out = outs.pop(0)
                for p in planes:
                    out[p] = merged[p]
            else:
                lse = merged[0] + jnp.log2(merged[1])
                outs.pop(0)[...] = lse
                own = 2.0 * merged[2] if len(merged) > 2 else 0.0
                outs.pop(0)[...] = jnp.sum(lse - own, axis=0, keepdims=True) * loss_scale[k // 2]

    return vmem_call(kernel, out_shape, name, 0, 0, [], *arrays)


def join_call(parts, name):
    def kernel(*refs):
        at = 0
        for ref in refs[:-1]:
            refs[-1][pl.ds(at, ref.shape[0]), :] = ref[...]
            at += ref.shape[0]

    return vmem_call(kernel, [bf16(sum(p.shape[0] for p in parts), parts[0].shape[1])], name, 0, 0, [], *parts)[0]


def soft_weights(v, row_lse, col_lse, first_id, col_ids):
    ids = first_id + lax.broadcasted_iota(jnp.int32, (v.shape[0], 1), 0)
    soft = 0.5 * (jnp.exp2(v - to_rows(row_lse)) + jnp.exp2(v - col_lse))
    return (soft - jnp.where(ids == col_ids, 1.0, 0.0)).astype(jnp.bfloat16)


def weight_steps(w_ref, s_ref, row_ref, col_ref, place, h, rows):
    slots = range(col_ref.shape[0])
    col_lse = jnp.concatenate([col_ref[pl.ds(k, 1), :] for k in slots], axis=1)
    within = lax.broadcasted_iota(jnp.int32, (1, rows), 1)
    col_ids = jnp.concatenate([text_block(place, k) * rows + within for k in slots], axis=1)
    first = h * 2 * RING

    def weights(i):
        for j in range(TILE_SLOTS):
            slot = i * TILE_SLOTS + j
            at = pl.ds(slot * rows, rows)
            w_ref[at, :] = soft_weights(
                s_ref[at, :], row_ref[pl.ds(first + slot, 1), :], col_lse, image_block(place, h, slot) * rows, col_ids)

    return weights


def put_digits(part_ref, loss_ref, rows):
    left = jnp.sum(loss_ref[...], axis=1, keepdims=True)
    number = lax.broadcasted_iota(jnp.int32, (EXTRA, 1), 0)
    block = jnp.zeros((EXTRA, 1), jnp.float32)
    for k, unit in enumerate(UNITS):
        digit = jnp.floor(left * (1.0 / unit) + 0.5)
        left = left - digit * unit
        block = jnp.where(number == k, digit, block)
    for slot in range(part_ref.shape[0]):
        part_ref[slot, pl.ds(rows, EXTRA), :] = jnp.broadcast_to(block, (EXTRA, part_ref.shape[2]))


def put_slots(own_ref, other_ref, slot, part, rows):
    for j in range(part.shape[0] // rows):
        out = own_ref if slot + j < RING else other_ref
        out[(slot + j) % RING, pl.ds(0, rows), :] = part[j * rows:(j + 1) * rows]


def image_call(s, row_lse, col_lse, loss, place, h, text, rows, name):
    m, n = s.shape
    width = text.shape[1]

    def kernel(*refs):
        place, refs = place_refs(refs), refs[len(AXES):]
        s_ref, row_ref, col_ref, loss_ref, t_ref, w_ref, own_ref, other_ref = refs
        tile = rows * TILE_SLOTS
        tiles = m // tile
        weights = weight_steps(w_ref, s_ref, row_ref, col_ref, place, h, rows)
        put_digits(own_ref, loss_ref, rows)
        other_ref[:, pl.ds(rows, EXTRA), :] = own_ref[:, pl.ds(rows, EXTRA), :]

        def dots(i):
            put_slots(own_ref, other_ref, i * TILE_SLOTS, jnp.dot(
                w_ref[pl.ds(i * tile, tile), :], t_ref[...], preferred_element_type=jnp.float32), rows)

        weights(0)
        for i in range(tiles):
            if i + 1 < tiles:
                weights(i + 1)
            dots(i)

    parts = [f32(RING, rows + EXTRA, width)] * 2
    return vmem_call(kernel, [bf16(m, n)] + parts, name, 2 * m * n * width, 2 * m * n,
                     place, s, row_lse, col_lse, loss, text)


def text_columns(first, n, rows):
    lo = first * rows // 128 * 128
    hi = min(n, -(-(first + RING) * rows // 128) * 128)
    return pl.ds(lo, hi - lo), first * rows - lo


def text_call(w_near, x_near, w_far, x_far, loss, first, rows, name):
    m, n = w_near.shape
    width = x_near.shape[1]
    chunk = 384

    def kernel(wn_ref, xn_ref, wf_ref, xf_ref, loss_ref, part_ref):
        dims = (((0,), (0,)), ((), ()))
        columns, lead = text_columns(first, n, rows)
        put_digits(part_ref, loss_ref, rows)
        for j in range(width // chunk):
            at = pl.ds(j * chunk, chunk)
            part = (lax.dot_general(wf_ref[:, columns], xf_ref[:, at], dims, preferred_element_type=jnp.float32)
                    + lax.dot_general(wn_ref[:, columns], xn_ref[:, at], dims, preferred_element_type=jnp.float32))
            for k in range(RING):
                part_ref[k, pl.ds(0, rows), at] = part[lead + k * rows:lead + (k + 1) * rows]

    return vmem_call(kernel, [f32(RING, rows + EXTRA, width)], name, 2 * m * n * width, 0, [],
                     w_near, x_near, w_far, x_far, loss)[0]


def after(value, *others):
    return lax.optimization_barrier((value, *others))[0]


def ring_shift(value, axis, step):
    return lax.ppermute(value, axis, [(i, (i + step) % RING) for i in range(RING)])


def ring_split(value, axis, sign):
    pairs = []
    for i in range(RING):
        for core in range(2):
            target = (i + (sign if core == 0 else -sign)) % RING
            pairs.append((i * 2 + core, target * 2 + core))
    return lax.ppermute(value, (axis, "core"), pairs)


def swap(value, axis):
    return lax.ppermute(value, axis, [(0, 1), (1, 0)])


def ring_gather(value, axis, first_core, wait_for=None):
    one = ring_shift(value, axis, 1)
    three = ring_shift(value, axis, 3)
    two = ring_split(jnp.where(first_core, one, three if wait_for is None else after(three, wait_for)), axis, 1)
    return [value, one, two, three]


def summed(own, other):
    return own + other.astype(jnp.float32)


def ring_outgoing(one, three, through, first_core):
    through = through.astype(jnp.float32)
    left = one + jnp.where(first_core, through, 0.0)
    right = three + jnp.where(first_core, 0.0, through)
    return left.astype(jnp.float16), right.astype(jnp.float16)


def ring_arrived(own, left, right, axis):
    return own + ring_shift(left, axis, -1).astype(jnp.float32) + ring_shift(right, axis, 1).astype(jnp.float32)


def on_device(image, text, log_scale):
    inverse_temp = jnp.exp(log_scale)
    rows = image.shape[0]
    core = lax.axis_index("core")
    place = [lax.axis_index(axis).reshape(1) for axis in AXES]
    scale = (inverse_temp * jnp.float32(math.log2(math.e))).reshape(1)
    image, text, scale, place, first_core = lax.optimization_barrier((image, text, scale, place, core == 0))

    text_far = swap(text, "ylo")
    image_far = swap(image, "yhi")
    text_near_slots = ring_gather(text, "z", first_core)
    text_near = join_call(text_near_slots, "join_text")
    text_far_slots = ring_gather(text_far, "z", first_core, text_near)
    image_near_slots = ring_gather(image, "x", first_core)
    image_far_slots = ring_gather(image_far, "x", first_core)
    image_near = join_call(image_near_slots, "join_image")
    image_near_other = swap(image_near, "core")
    image_far_other = [swap(a, "core") for a in image_far_slots]

    s_near, x_near, row_stat, col_stat, t_all = score_call(
        [image_near, image_near_other], [text_near] + text_far_slots, scale, place, 0, [], rows, "score_near")
    s_far, x_far, row_stat, col_stat = score_call(
        image_far_slots + image_far_other, [t_all], scale, place, 1, [row_stat, col_stat], rows, "score_far")

    loss_scale = math.log(2.0) / (2 * 128 * rows)
    one, two = (functools.partial(turned, step=step) for step in (1, 2))
    cores, pairs = functools.partial(swapped, group=RING), functools.partial(swapped, group=2 * RING)
    row_stat, col_stat = merge_call(
        row_stat, swap(row_stat, "core"), cores, col_stat, ring_shift(col_stat, "z", 1), one,
        (None, None), "merge_core")
    row_stat, col_stat = merge_call(
        row_stat, ring_shift(row_stat, "x", 1), one, col_stat, ring_shift(col_stat, "z", 2), two,
        (None, None), "merge_one")
    row_stat, col_lse, col_loss = merge_call(
        row_stat, ring_shift(row_stat, "x", 2), two, col_stat, swap(col_stat, "ylo"), cores,
        (None, loss_scale), "merge_two")
    row_lse, row_loss = merge_call(
        row_stat, swap(row_stat, "yhi"), pairs, None, None, None, (loss_scale,), "merge_pair")

    w_far, far_own, far_part = image_call(s_far, row_lse, col_lse, col_loss, place, 1, t_all, rows, "image_far")
    far_send = far_part.astype(jnp.float16)
    far_other = swap(far_send, "core")
    w_near, near_own, near_part = image_call(
        s_near, after(row_lse, far_send), col_lse, col_loss, place, 0, t_all, rows, "image_near")
    near_send = near_part.astype(jnp.float16)
    near_other = swap(near_send, "core")
    far_text = text_call(w_near, x_near, w_far, x_far, after(row_loss, near_send), RING, rows, "text_far")
    far_text_two = far_text[2].astype(jnp.float16)
    far_text_through = ring_split(far_text_two, "z", -1)
    other, _ = lax.optimization_barrier(((near_other, far_other), far_text_two))
    near_other, far_other = other
    image_two = jnp.stack([summed(near_own[2], near_other[2]), summed(far_own[2], far_other[2])]).astype(jnp.float16)
    image_through = ring_split(image_two, "x", -1)
    near_text = text_call(w_near, x_near, w_far, x_far, after(row_loss, image_two), 0, rows, "text_near")
    near_text_two = near_text[2].astype(jnp.float16)
    near_text_through = ring_split(near_text_two, "z", -1)

    text_left, text_right = ring_outgoing(
        far_text[1], far_text[3], after(far_text_through, near_text_two), first_core)
    far_left, far_right = ring_outgoing(
        summed(far_own[1], far_other[1]), summed(far_own[3], far_other[3]), after(image_through, text_left)[1], first_core)
    near_text_left, near_text_right = ring_outgoing(
        near_text[1], near_text[3], after(near_text_through, far_left), first_core)
    near_left, near_right = ring_outgoing(
        summed(near_own[1], near_other[1]), summed(near_own[3], near_other[3]),
        after(image_through, near_text_left)[0], first_core)
    text_far_sum = ring_arrived(after(far_text[0], near_left), text_left, text_right, "z").astype(jnp.float16)
    text_far_in = swap(text_far_sum, "ylo")
    image_far_sum = ring_arrived(
        summed(far_own[0], after(far_other, text_far_sum)[0]), far_left, far_right, "x").astype(jnp.float16)
    image_far_in = swap(image_far_sum, "yhi")
    image_sum = (ring_arrived(summed(near_own[0], after(near_other, image_far_sum)[0]), near_left, near_right, "x")
                 + image_far_in.astype(jnp.float32))
    text_sum = (ring_arrived(near_text[0], near_text_left, near_text_right, "z")
                + text_far_in.astype(jnp.float32))

    digits = text_sum[rows:, 0] + image_sum[rows:, 0]
    loss_value = sum(digits[k] * unit for k, unit in enumerate(UNITS))
    return loss_value, inverse_temp * image_sum[:rows], inverse_temp * text_sum[:rows]


def solution(mesh):
    fine = Mesh(mesh.devices.reshape(2, 4, 4, 2, 2), AXES)
    text_spec = P(("yhi", "core", "ylo", "z", "x"), None)
    return jax.shard_map(
        on_device, mesh=fine, in_specs=(P(AXES, None), text_spec, P()),
        out_specs=(P(), P(AXES, None), text_spec), check_vma=False
    )
```

```python
import functools
import math

import jax
import jax.numpy as jnp
from jax import lax
from jax.experimental import pallas as pl
from jax.experimental.pallas import tpu as pltpu
from jax.sharding import Mesh, PartitionSpec as P

AXES = ("ylo", "z", "x", "yhi", "core")
RING = 4
TILE_SLOTS = 2
EXTRA = 8
UNITS = (256.0, 1.0, 2.0 ** -8, 2.0 ** -16, 2.0 ** -24)
VMEM_LIMIT = 12 * 1024 * 1024


def f32(*shape):
    return jax.ShapeDtypeStruct(shape, jnp.float32)


def bf16(*shape):
    return jax.ShapeDtypeStruct(shape, jnp.bfloat16)


def vmem_call(kernel, out_shape, name, flops, transcendentals, scalars, *args):
    vmem = pl.BlockSpec(memory_space=pltpu.VMEM)
    nbytes = sum(a.size * a.dtype.itemsize for a in args)
    nbytes += sum(math.prod(o.shape) * o.dtype.itemsize for o in out_shape)
    return pl.pallas_call(
        kernel,
        in_specs=[pl.BlockSpec(memory_space=pltpu.SMEM)] * len(scalars) + [vmem] * len(args),
        out_specs=[vmem] * len(out_shape),
        out_shape=out_shape,
        compiler_params=pltpu.CompilerParams(vmem_limit_bytes=VMEM_LIMIT),
        cost_estimate=pl.CostEstimate(flops=flops, bytes_accessed=nbytes, transcendentals=transcendentals),
        name=name,
    )(*scalars, *args)


def to_lanes(column):
    return jnp.broadcast_to(column, (column.shape[0], 128)).T[0:1, :]


def to_rows(line):
    return jnp.broadcast_to(line, (128, line.shape[1])).T[:, 0:1]


def merge(stats):
    top = stats[0][0]
    for stat in stats[1:]:
        top = jnp.maximum(top, stat[0])
    total = sum(stat[1] * jnp.exp2(stat[0] - top) for stat in stats)
    return [top, total] + [sum(stat[k] for stat in stats) for k in range(2, len(stats[0]))]


def place_refs(refs):
    return {axis: refs[k][0] for k, axis in enumerate(AXES)}


def image_block(place, h, slot):
    x = lax.rem(place["x"] + RING - slot % RING, RING)
    core = place["core"] if slot < RING else 1 - place["core"]
    yhi = place["yhi"] if h == 0 else 1 - place["yhi"]
    return ((place["ylo"] * 4 + place["z"]) * 4 + x) * 4 + yhi * 2 + core


def text_block(place, slot):
    z = lax.rem(place["z"] + RING - slot % RING, RING)
    ylo = place["ylo"] if slot < RING else 1 - place["ylo"]
    return (place["yhi"] * 2 + place["core"]) * 32 + (ylo * 4 + z) * 4 + place["x"]


def score_call(images, texts, scale, place, h, near_stats, rows, name):
    width = images[0].shape[1]
    sizes = [a.shape[0] for a in images]
    text_sizes = [a.shape[0] for a in texts]
    m, n = sum(sizes), sum(text_sizes)
    slots = m // rows
    before = near_stats[0].shape[1] if near_stats else 0
    keep_text = len(texts) > 1

    def kernel(scale_ref, *refs):
        place, refs = place_refs(refs), refs[len(AXES):]
        image_refs, refs = refs[:len(images)], refs[len(images):]
        text_refs, refs = refs[:len(texts)], refs[len(texts):]
        held, refs = refs[:len(near_stats)], refs[len(near_stats):]
        s_ref, x_ref, row_ref, col_ref = refs[:4]
        t_ref = refs[4] if keep_text else text_refs[0]

        def fill(target, sources, counts):
            at = 0
            for source, count in zip(sources, counts):
                target[pl.ds(at, count), :] = source[...]
                at += count

        if keep_text:
            fill(t_ref, text_refs, text_sizes)
        fill(x_ref, image_refs, sizes)
        tile = rows * TILE_SLOTS
        tiles = m // tile
        scale = scale_ref[0]
        col_parts = []

        def scores(i):
            s_ref[pl.ds(i * tile, tile), :] = scale * lax.dot_general(
                x_ref[pl.ds(i * tile, tile), :], t_ref[...], (((1,), (1,)), ((), ())),
                preferred_element_type=jnp.float32)

        def stats(i):
            s = s_ref[pl.ds(i * tile, tile), :]
            col_top = jnp.max(s, axis=0, keepdims=True)
            col_parts.append((col_top, jnp.sum(jnp.exp2(s - col_top), axis=0, keepdims=True)))
            for j in range(TILE_SLOTS):
                slot = i * TILE_SLOTS + j
                s = s_ref[pl.ds(slot * rows, rows), :]
                row_top = jnp.max(s, axis=1, keepdims=True)
                row_sum = jnp.sum(jnp.exp2(s - row_top), axis=1, keepdims=True)
                row_ref[0, pl.ds(before + slot, 1), :] = to_lanes(row_top)
                row_ref[1, pl.ds(before + slot, 1), :] = to_lanes(row_sum)

        scores(0)
        for i in range(tiles):
            if i + 1 < tiles:
                scores(i + 1)
            stats(i)
        top, total = merge(col_parts)
        for k in range(n // rows):
            at = slice(k * rows, (k + 1) * rows)
            part = [(top[:, at], total[:, at])]
            if held:
                part.append((held[1][0, pl.ds(k, 1), :], held[1][1, pl.ds(k, 1), :]))
            col_ref[0, pl.ds(k, 1), :], col_ref[1, pl.ds(k, 1), :] = merge(part)
        if held:
            row_ref[:, pl.ds(0, before), :] = held[0][...]
        row_ref[2, pl.ds(before, slots), :] = jnp.zeros((slots, rows), jnp.float32)
        for slot in range(slots):
            for k in range(n // rows):
                @pl.when(image_block(place, h, slot) == text_block(place, k))
                def _():
                    s = s_ref[pl.ds(slot * rows, rows), :][:, k * rows:(k + 1) * rows]
                    mask = (lax.broadcasted_iota(jnp.int32, (rows, 1), 0)
                            == lax.broadcasted_iota(jnp.int32, (1, rows), 1))
                    row_ref[2, pl.ds(before + slot, 1), :] = jnp.sum(jnp.where(mask, s, 0.0), axis=0, keepdims=True)

    out_shape = [f32(m, n), bf16(m, width), f32(3, before + slots, rows), f32(2, n // rows, rows)]
    out_shape += [bf16(n, width)] * keep_text
    return vmem_call(kernel, out_shape, name, 2 * m * n * width, 2 * m * n, [scale, *place],
                     *images, *texts, *near_stats)


def turned(ref, k, step):
    rings = []
    for lo in range(0, ref.shape[1], RING):
        rings.append(ref[k, pl.ds(lo + RING - step, step), :])
        rings.append(ref[k, pl.ds(lo, RING - step), :])
    return jnp.concatenate(rings, axis=0)


def swapped(ref, k, group):
    parts = []
    for lo in range(0, ref.shape[1], 2 * group):
        parts.append(ref[k, pl.ds(lo + group, group), :])
        parts.append(ref[k, pl.ds(lo, group), :])
    return jnp.concatenate(parts, axis=0)


def merge_call(row, row_in, row_order, col, col_in, col_order, loss_scale, name):
    arrays = [row, row_in] + ([] if col is None else [col, col_in])
    pairs = [(row, row_order, 0)] + ([] if col is None else [(col, col_order, 2)])
    out_shape = []
    for stat, _, k in pairs:
        done = loss_scale[k // 2] is not None
        out_shape += [f32(*stat.shape[1:]), f32(1, stat.shape[2])] if done else [f32(*stat.shape)]

    def kernel(*refs):
        outs = list(refs[len(arrays):])
        for stat, order, k in pairs:
            planes = range(stat.shape[0])
            merged = merge([[refs[k][p] for p in planes], [order(refs[k + 1], p) for p in planes]])
            if loss_scale[k // 2] is None:
                out = outs.pop(0)
                for p in planes:
                    out[p] = merged[p]
            else:
                lse = merged[0] + jnp.log2(merged[1])
                outs.pop(0)[...] = lse
                own = 2.0 * merged[2] if len(merged) > 2 else 0.0
                outs.pop(0)[...] = jnp.sum(lse - own, axis=0, keepdims=True) * loss_scale[k // 2]

    return vmem_call(kernel, out_shape, name, 0, 0, [], *arrays)


def join_call(parts, name):
    def kernel(*refs):
        at = 0
        for ref in refs[:-1]:
            refs[-1][pl.ds(at, ref.shape[0]), :] = ref[...]
            at += ref.shape[0]

    return vmem_call(kernel, [bf16(sum(p.shape[0] for p in parts), parts[0].shape[1])], name, 0, 0, [], *parts)[0]


def soft_weights(v, row_lse, col_lse, first_id, col_ids):
    ids = first_id + lax.broadcasted_iota(jnp.int32, (v.shape[0], 1), 0)
    soft = 0.5 * (jnp.exp2(v - to_rows(row_lse)) + jnp.exp2(v - col_lse))
    return (soft - jnp.where(ids == col_ids, 1.0, 0.0)).astype(jnp.bfloat16)


def weight_steps(w_ref, s_ref, row_ref, col_ref, place, h, rows):
    slots = range(col_ref.shape[0])
    col_lse = jnp.concatenate([col_ref[pl.ds(k, 1), :] for k in slots], axis=1)
    within = lax.broadcasted_iota(jnp.int32, (1, rows), 1)
    col_ids = jnp.concatenate([text_block(place, k) * rows + within for k in slots], axis=1)
    first = h * 2 * RING

    def weights(i):
        for j in range(TILE_SLOTS):
            slot = i * TILE_SLOTS + j
            at = pl.ds(slot * rows, rows)
            w_ref[at, :] = soft_weights(
                s_ref[at, :], row_ref[pl.ds(first + slot, 1), :], col_lse, image_block(place, h, slot) * rows, col_ids)

    return weights


def put_digits(part_ref, loss_ref, rows):
    left = jnp.sum(loss_ref[...], axis=1, keepdims=True)
    number = lax.broadcasted_iota(jnp.int32, (EXTRA, 1), 0)
    block = jnp.zeros((EXTRA, 1), jnp.float32)
    for k, unit in enumerate(UNITS):
        digit = jnp.floor(left * (1.0 / unit) + 0.5)
        left = left - digit * unit
        block = jnp.where(number == k, digit, block)
    for slot in range(part_ref.shape[0]):
        part_ref[slot, pl.ds(rows, EXTRA), :] = jnp.broadcast_to(block, (EXTRA, part_ref.shape[2]))


def put_slots(own_ref, other_ref, slot, part, rows):
    for j in range(part.shape[0] // rows):
        out = own_ref if slot + j < RING else other_ref
        out[(slot + j) % RING, pl.ds(0, rows), :] = part[j * rows:(j + 1) * rows]


def image_call(s, row_lse, col_lse, loss, place, h, text, rows, name):
    m, n = s.shape
    width = text.shape[1]

    def kernel(*refs):
        place, refs = place_refs(refs), refs[len(AXES):]
        s_ref, row_ref, col_ref, loss_ref, t_ref, w_ref, own_ref, other_ref = refs
        tile = rows * TILE_SLOTS
        tiles = m // tile
        weights = weight_steps(w_ref, s_ref, row_ref, col_ref, place, h, rows)
        put_digits(own_ref, loss_ref, rows)
        other_ref[:, pl.ds(rows, EXTRA), :] = own_ref[:, pl.ds(rows, EXTRA), :]

        def dots(i):
            put_slots(own_ref, other_ref, i * TILE_SLOTS, jnp.dot(
                w_ref[pl.ds(i * tile, tile), :], t_ref[...], preferred_element_type=jnp.float32), rows)

        weights(0)
        for i in range(tiles):
            if i + 1 < tiles:
                weights(i + 1)
            dots(i)

    parts = [f32(RING, rows + EXTRA, width)] * 2
    return vmem_call(kernel, [bf16(m, n)] + parts, name, 2 * m * n * width, 2 * m * n,
                     place, s, row_lse, col_lse, loss, text)


def text_columns(first, n, rows):
    lo = first * rows // 128 * 128
    hi = min(n, -(-(first + RING) * rows // 128) * 128)
    return pl.ds(lo, hi - lo), first * rows - lo


def text_call(w_near, x_near, w_far, x_far, loss, first, rows, name):
    m, n = w_near.shape
    width = x_near.shape[1]
    chunk = 384

    def kernel(wn_ref, xn_ref, wf_ref, xf_ref, loss_ref, part_ref):
        dims = (((0,), (0,)), ((), ()))
        columns, lead = text_columns(first, n, rows)
        put_digits(part_ref, loss_ref, rows)
        for j in range(width // chunk):
            at = pl.ds(j * chunk, chunk)
            part = (lax.dot_general(wf_ref[:, columns], xf_ref[:, at], dims, preferred_element_type=jnp.float32)
                    + lax.dot_general(wn_ref[:, columns], xn_ref[:, at], dims, preferred_element_type=jnp.float32))
            for k in range(RING):
                part_ref[k, pl.ds(0, rows), at] = part[lead + k * rows:lead + (k + 1) * rows]

    return vmem_call(kernel, [f32(RING, rows + EXTRA, width)], name, 2 * m * n * width, 0, [],
                     w_near, x_near, w_far, x_far, loss)[0]


def after(value, *others):
    return lax.optimization_barrier((value, *others))[0]


def ring_shift(value, axis, step):
    return lax.ppermute(value, axis, [(i, (i + step) % RING) for i in range(RING)])


def ring_split(value, axis, sign):
    pairs = []
    for i in range(RING):
        for core in range(2):
            target = (i + (sign if core == 0 else -sign)) % RING
            pairs.append((i * 2 + core, target * 2 + core))
    return lax.ppermute(value, (axis, "core"), pairs)


def swap(value, axis):
    return lax.ppermute(value, axis, [(0, 1), (1, 0)])


def ring_gather(value, axis, first_core, wait_for=None):
    one = ring_shift(value, axis, 1)
    three = ring_shift(value, axis, 3)
    two = ring_split(jnp.where(first_core, one, three if wait_for is None else after(three, wait_for)), axis, 1)
    return [value, one, two, three]


def summed(own, other):
    return own + other.astype(jnp.float32)


def ring_outgoing(one, three, through, first_core):
    through = through.astype(jnp.float32)
    left = one + jnp.where(first_core, through, 0.0)
    right = three + jnp.where(first_core, 0.0, through)
    return left.astype(jnp.float16), right.astype(jnp.float16)


def ring_arrived(own, left, right, axis):
    return own + ring_shift(left, axis, -1).astype(jnp.float32) + ring_shift(right, axis, 1).astype(jnp.float32)


def on_device(image, text, log_scale):
    inverse_temp = jnp.exp(log_scale)
    rows = image.shape[0]
    core = lax.axis_index("core")
    place = [lax.axis_index(axis).reshape(1) for axis in AXES]
    scale = (inverse_temp * jnp.float32(math.log2(math.e))).reshape(1)
    image, text, scale, place, first_core = lax.optimization_barrier((image, text, scale, place, core == 0))

    text_far = swap(text, "ylo")
    image_far = swap(image, "yhi")
    text_near_slots = ring_gather(text, "z", first_core)
    text_near = join_call(text_near_slots, "join_text")
    text_far_slots = ring_gather(text_far, "z", first_core, text_near)
    image_near_slots = ring_gather(image, "x", first_core)
    image_far_slots = ring_gather(image_far, "x", first_core)
    image_near = join_call(image_near_slots, "join_image")
    image_near_other = swap(image_near, "core")
    image_far_other = [swap(a, "core") for a in image_far_slots]

    s_near, x_near, row_stat, col_stat, t_all = score_call(
        [image_near, image_near_other], [text_near] + text_far_slots, scale, place, 0, [], rows, "score_near")
    s_far, x_far, row_stat, col_stat = score_call(
        image_far_slots + image_far_other, [t_all], scale, place, 1, [row_stat, col_stat], rows, "score_far")

    loss_scale = math.log(2.0) / (2 * 128 * rows)
    one, two = (functools.partial(turned, step=step) for step in (1, 2))
    cores, pairs = functools.partial(swapped, group=RING), functools.partial(swapped, group=2 * RING)
    row_stat, col_stat = merge_call(
        row_stat, swap(row_stat, "core"), cores, col_stat, ring_shift(col_stat, "z", 1), one,
        (None, None), "merge_core")
    row_stat, col_stat = merge_call(
        row_stat, ring_shift(row_stat, "x", 1), one, col_stat, ring_shift(col_stat, "z", 2), two,
        (None, None), "merge_one")
    row_stat, col_lse, col_loss = merge_call(
        row_stat, ring_shift(row_stat, "x", 2), two, col_stat, swap(col_stat, "ylo"), cores,
        (None, loss_scale), "merge_two")
    row_lse, row_loss = merge_call(
        row_stat, swap(row_stat, "yhi"), pairs, None, None, None, (loss_scale,), "merge_pair")

    w_far, far_own, far_part = image_call(s_far, row_lse, col_lse, col_loss, place, 1, t_all, rows, "image_far")
    far_send = far_part.astype(jnp.float16)
    far_other = swap(far_send, "core")
    w_near, near_own, near_part = image_call(
        s_near, after(row_lse, far_send), col_lse, col_loss, place, 0, t_all, rows, "image_near")
    near_send = near_part.astype(jnp.float16)
    near_other = swap(near_send, "core")
    far_text = text_call(w_near, x_near, w_far, x_far, after(row_loss, near_send), RING, rows, "text_far")
    far_text_two = far_text[2].astype(jnp.float16)
    far_text_through = ring_split(far_text_two, "z", -1)
    other, _ = lax.optimization_barrier(((near_other, far_other), far_text_two))
    near_other, far_other = other
    image_two = jnp.stack([summed(near_own[2], near_other[2]), summed(far_own[2], far_other[2])]).astype(jnp.float16)
    image_through = ring_split(image_two, "x", -1)
    near_text = text_call(w_near, x_near, w_far, x_far, after(row_loss, image_two), 0, rows, "text_near")
    near_text_two = near_text[2].astype(jnp.float16)
    near_text_through = ring_split(near_text_two, "z", -1)

    text_left, text_right = ring_outgoing(
        far_text[1], far_text[3], after(far_text_through, near_text_two), first_core)
    far_left, far_right = ring_outgoing(
        summed(far_own[1], far_other[1]), summed(far_own[3], far_other[3]), after(image_through, text_left)[1], first_core)
    near_text_left, near_text_right = ring_outgoing(
        near_text[1], near_text[3], after(near_text_through, far_left), first_core)
    near_left, near_right = ring_outgoing(
        summed(near_own[1], near_other[1]), summed(near_own[3], near_other[3]),
        after(image_through, near_text_left)[0], first_core)
    text_far_sum = ring_arrived(after(far_text[0], near_left), text_left, text_right, "z").astype(jnp.float16)
    text_far_in = swap(text_far_sum, "ylo")
    image_far_sum = ring_arrived(
        summed(far_own[0], after(far_other, text_far_sum)[0]), far_left, far_right, "x").astype(jnp.float16)
    image_far_in = swap(image_far_sum, "yhi")
    image_sum = (ring_arrived(summed(near_own[0], after(near_other, image_far_sum)[0]), near_left, near_right, "x")
                 + image_far_in.astype(jnp.float32))
    text_sum = (ring_arrived(near_text[0], near_text_left, near_text_right, "z")
                + text_far_in.astype(jnp.float32))

    digits = text_sum[rows:, 0] + image_sum[rows:, 0]
    loss_value = sum(digits[k] * unit for k, unit in enumerate(UNITS))
    return loss_value, inverse_temp * image_sum[:rows], inverse_temp * text_sum[:rows]


def solution(mesh):
    fine = Mesh(mesh.devices.reshape(2, 4, 4, 2, 2), AXES)
    text_spec = P(("yhi", "core", "ylo", "z", "x"), None)
    return jax.shard_map(
        on_device, mesh=fine, in_specs=(P(AXES, None), text_spec, P()),
        out_specs=(P(), P(AXES, None), text_spec), check_vma=False
    )
```

```python
import functools
import math

import jax
import jax.numpy as jnp
from jax import lax
from jax.experimental import pallas as pl
from jax.experimental.pallas import tpu as pltpu
from jax.sharding import Mesh, PartitionSpec as P

AXES = ("ylo", "z", "x", "yhi", "core")
RING = 4
TILE_SLOTS = 2
EXTRA = 8
UNITS = (256.0, 1.0, 2.0 ** -8, 2.0 ** -16, 2.0 ** -24)
VMEM_LIMIT = 12 * 1024 * 1024


def f32(*shape):
    return jax.ShapeDtypeStruct(shape, jnp.float32)


def bf16(*shape):
    return jax.ShapeDtypeStruct(shape, jnp.bfloat16)


def vmem_call(kernel, out_shape, name, flops, transcendentals, scalars, *args):
    vmem = pl.BlockSpec(memory_space=pltpu.VMEM)
    nbytes = sum(a.size * a.dtype.itemsize for a in args)
    nbytes += sum(math.prod(o.shape) * o.dtype.itemsize for o in out_shape)
    return pl.pallas_call(
        kernel,
        in_specs=[pl.BlockSpec(memory_space=pltpu.SMEM)] * len(scalars) + [vmem] * len(args),
        out_specs=[vmem] * len(out_shape),
        out_shape=out_shape,
        compiler_params=pltpu.CompilerParams(vmem_limit_bytes=VMEM_LIMIT),
        cost_estimate=pl.CostEstimate(flops=flops, bytes_accessed=nbytes, transcendentals=transcendentals),
        name=name,
    )(*scalars, *args)


def to_lanes(column):
    return jnp.broadcast_to(column, (column.shape[0], 128)).T[0:1, :]


def to_rows(line):
    return jnp.broadcast_to(line, (128, line.shape[1])).T[:, 0:1]


def merge(stats):
    top = stats[0][0]
    for stat in stats[1:]:
        top = jnp.maximum(top, stat[0])
    total = sum(stat[1] * jnp.exp2(stat[0] - top) for stat in stats)
    return [top, total] + [sum(stat[k] for stat in stats) for k in range(2, len(stats[0]))]


def place_refs(refs):
    return {axis: refs[k][0] for k, axis in enumerate(AXES)}


def image_block(place, h, slot):
    x = lax.rem(place["x"] + RING - slot % RING, RING)
    core = place["core"] if slot < RING else 1 - place["core"]
    yhi = place["yhi"] if h == 0 else 1 - place["yhi"]
    return ((place["ylo"] * 4 + place["z"]) * 4 + x) * 4 + yhi * 2 + core


def text_block(place, slot):
    z = lax.rem(place["z"] + RING - slot % RING, RING)
    ylo = place["ylo"] if slot < RING else 1 - place["ylo"]
    return (place["yhi"] * 2 + place["core"]) * 32 + (ylo * 4 + z) * 4 + place["x"]


def score_call(images, texts, scale, place, h, near_stats, rows, name):
    width = images[0].shape[1]
    sizes = [a.shape[0] for a in images]
    text_sizes = [a.shape[0] for a in texts]
    m, n = sum(sizes), sum(text_sizes)
    slots = m // rows
    before = near_stats[0].shape[1] if near_stats else 0
    keep_text = len(texts) > 1

    def kernel(scale_ref, *refs):
        place, refs = place_refs(refs), refs[len(AXES):]
        image_refs, refs = refs[:len(images)], refs[len(images):]
        text_refs, refs = refs[:len(texts)], refs[len(texts):]
        held, refs = refs[:len(near_stats)], refs[len(near_stats):]
        s_ref, x_ref, row_ref, col_ref = refs[:4]
        t_ref = refs[4] if keep_text else text_refs[0]

        def fill(target, sources, counts):
            at = 0
            for source, count in zip(sources, counts):
                target[pl.ds(at, count), :] = source[...]
                at += count

        if keep_text:
            fill(t_ref, text_refs, text_sizes)
        fill(x_ref, image_refs, sizes)
        tile = rows * TILE_SLOTS
        tiles = m // tile
        scale = scale_ref[0]
        col_parts = []

        def scores(i):
            s_ref[pl.ds(i * tile, tile), :] = scale * lax.dot_general(
                x_ref[pl.ds(i * tile, tile), :], t_ref[...], (((1,), (1,)), ((), ())),
                preferred_element_type=jnp.float32)

        def stats(i):
            s = s_ref[pl.ds(i * tile, tile), :]
            col_top = jnp.max(s, axis=0, keepdims=True)
            col_parts.append((col_top, jnp.sum(jnp.exp2(s - col_top), axis=0, keepdims=True)))
            for j in range(TILE_SLOTS):
                slot = i * TILE_SLOTS + j
                s = s_ref[pl.ds(slot * rows, rows), :]
                row_top = jnp.max(s, axis=1, keepdims=True)
                row_sum = jnp.sum(jnp.exp2(s - row_top), axis=1, keepdims=True)
                row_ref[0, pl.ds(before + slot, 1), :] = to_lanes(row_top)
                row_ref[1, pl.ds(before + slot, 1), :] = to_lanes(row_sum)

        scores(0)
        for i in range(tiles):
            if i + 1 < tiles:
                scores(i + 1)
            stats(i)
        top, total = merge(col_parts)
        for k in range(n // rows):
            at = slice(k * rows, (k + 1) * rows)
            part = [(top[:, at], total[:, at])]
            if held:
                part.append((held[1][0, pl.ds(k, 1), :], held[1][1, pl.ds(k, 1), :]))
            col_ref[0, pl.ds(k, 1), :], col_ref[1, pl.ds(k, 1), :] = merge(part)
        if held:
            row_ref[:, pl.ds(0, before), :] = held[0][...]
        row_ref[2, pl.ds(before, slots), :] = jnp.zeros((slots, rows), jnp.float32)
        for slot in range(slots):
            for k in range(n // rows):
                @pl.when(image_block(place, h, slot) == text_block(place, k))
                def _():
                    s = s_ref[pl.ds(slot * rows, rows), :][:, k * rows:(k + 1) * rows]
                    mask = (lax.broadcasted_iota(jnp.int32, (rows, 1), 0)
                            == lax.broadcasted_iota(jnp.int32, (1, rows), 1))
                    row_ref[2, pl.ds(before + slot, 1), :] = jnp.sum(jnp.where(mask, s, 0.0), axis=0, keepdims=True)

    out_shape = [f32(m, n), bf16(m, width), f32(3, before + slots, rows), f32(2, n // rows, rows)]
    out_shape += [bf16(n, width)] * keep_text
    return vmem_call(kernel, out_shape, name, 2 * m * n * width, 2 * m * n, [scale, *place],
                     *images, *texts, *near_stats)


def turned(ref, k, step):
    rings = []
    for lo in range(0, ref.shape[1], RING):
        rings.append(ref[k, pl.ds(lo + RING - step, step), :])
        rings.append(ref[k, pl.ds(lo, RING - step), :])
    return jnp.concatenate(rings, axis=0)


def swapped(ref, k, group):
    parts = []
    for lo in range(0, ref.shape[1], 2 * group):
        parts.append(ref[k, pl.ds(lo + group, group), :])
        parts.append(ref[k, pl.ds(lo, group), :])
    return jnp.concatenate(parts, axis=0)


def merge_call(row, row_in, col, col_in, loss_scale, name):
    arrays, out_shape = [], []
    for stat, came, scale in zip((row, col), (row_in, col_in), loss_scale):
        arrays += [stat] + [array for array, _ in came]
        out_shape += [f32(*stat.shape)] if scale is None else [f32(*stat.shape[1:]), f32(1, stat.shape[2])]

    def kernel(*refs):
        ins, outs = list(refs[:len(arrays)]), list(refs[len(arrays):])
        for stat, came, scale in zip((row, col), (row_in, col_in), loss_scale):
            planes = range(stat.shape[0])
            own = ins.pop(0)
            stats = [[own[p] for p in planes]]
            for _, order in came:
                ref = ins.pop(0)
                stats.append([order(ref, p) for p in planes])
            merged = merge(stats)
            if scale is None:
                out = outs.pop(0)
                for p in planes:
                    out[p] = merged[p]
            else:
                lse = merged[0] + jnp.log2(merged[1])
                outs.pop(0)[...] = lse
                diag = 2.0 * merged[2] if len(merged) > 2 else 0.0
                outs.pop(0)[...] = jnp.sum(lse - diag, axis=0, keepdims=True) * scale

    return vmem_call(kernel, out_shape, name, 0, 0, [], *arrays)


def join_call(parts, name):
    def kernel(*refs):
        at = 0
        for ref in refs[:-1]:
            refs[-1][pl.ds(at, ref.shape[0]), :] = ref[...]
            at += ref.shape[0]

    return vmem_call(kernel, [bf16(sum(p.shape[0] for p in parts), parts[0].shape[1])], name, 0, 0, [], *parts)[0]


def soft_weights(v, row_lse, col_lse, first_id, col_ids):
    ids = first_id + lax.broadcasted_iota(jnp.int32, (v.shape[0], 1), 0)
    soft = 0.5 * (jnp.exp2(v - to_rows(row_lse)) + jnp.exp2(v - col_lse))
    return (soft - jnp.where(ids == col_ids, 1.0, 0.0)).astype(jnp.bfloat16)


def weight_steps(w_ref, s_ref, row_ref, col_ref, place, h, rows):
    slots = range(col_ref.shape[0])
    col_lse = jnp.concatenate([col_ref[pl.ds(k, 1), :] for k in slots], axis=1)
    within = lax.broadcasted_iota(jnp.int32, (1, rows), 1)
    col_ids = jnp.concatenate([text_block(place, k) * rows + within for k in slots], axis=1)
    first = h * 2 * RING

    def weights(i):
        for j in range(TILE_SLOTS):
            slot = i * TILE_SLOTS + j
            at = pl.ds(slot * rows, rows)
            w_ref[at, :] = soft_weights(
                s_ref[at, :], row_ref[pl.ds(first + slot, 1), :], col_lse, image_block(place, h, slot) * rows, col_ids)

    return weights


def put_digits(part_ref, loss_ref, rows):
    left = jnp.sum(loss_ref[...], axis=1, keepdims=True)
    number = lax.broadcasted_iota(jnp.int32, (EXTRA, 1), 0)
    block = jnp.zeros((EXTRA, 1), jnp.float32)
    for k, unit in enumerate(UNITS):
        digit = jnp.floor(left * (1.0 / unit) + 0.5)
        left = left - digit * unit
        block = jnp.where(number == k, digit, block)
    for slot in range(part_ref.shape[0]):
        part_ref[slot, pl.ds(rows, EXTRA), :] = jnp.broadcast_to(block, (EXTRA, part_ref.shape[2]))


def put_slots(own_ref, other_ref, slot, part, rows):
    for j in range(part.shape[0] // rows):
        out = own_ref if slot + j < RING else other_ref
        out[(slot + j) % RING, pl.ds(0, rows), :] = part[j * rows:(j + 1) * rows]


def image_call(s, row_lse, col_lse, loss, place, h, text, rows, name):
    m, n = s.shape
    width = text.shape[1]

    def kernel(*refs):
        place, refs = place_refs(refs), refs[len(AXES):]
        s_ref, row_ref, col_ref, loss_ref, t_ref, w_ref, own_ref, other_ref = refs
        tile = rows * TILE_SLOTS
        tiles = m // tile
        weights = weight_steps(w_ref, s_ref, row_ref, col_ref, place, h, rows)
        put_digits(own_ref, loss_ref, rows)
        other_ref[:, pl.ds(rows, EXTRA), :] = own_ref[:, pl.ds(rows, EXTRA), :]

        def dots(i):
            put_slots(own_ref, other_ref, i * TILE_SLOTS, jnp.dot(
                w_ref[pl.ds(i * tile, tile), :], t_ref[...], preferred_element_type=jnp.float32), rows)

        weights(0)
        for i in range(tiles):
            if i + 1 < tiles:
                weights(i + 1)
            dots(i)

    parts = [f32(RING, rows + EXTRA, width)] * 2
    return vmem_call(kernel, [bf16(m, n)] + parts, name, 2 * m * n * width, 2 * m * n,
                     place, s, row_lse, col_lse, loss, text)


def text_columns(first, n, rows):
    lo = first * rows // 128 * 128
    hi = min(n, -(-(first + RING) * rows // 128) * 128)
    return pl.ds(lo, hi - lo), first * rows - lo


def text_call(w_near, x_near, w_far, x_far, loss, first, rows, name):
    m, n = w_near.shape
    width = x_near.shape[1]
    chunk = width

    def kernel(wn_ref, xn_ref, wf_ref, xf_ref, loss_ref, part_ref):
        dims = (((0,), (0,)), ((), ()))
        columns, lead = text_columns(first, n, rows)
        put_digits(part_ref, loss_ref, rows)
        for j in range(width // chunk):
            at = pl.ds(j * chunk, chunk)
            part = (lax.dot_general(wf_ref[:, columns], xf_ref[:, at], dims, preferred_element_type=jnp.float32)
                    + lax.dot_general(wn_ref[:, columns], xn_ref[:, at], dims, preferred_element_type=jnp.float32))
            for k in range(RING):
                part_ref[k, pl.ds(0, rows), at] = part[lead + k * rows:lead + (k + 1) * rows]

    return vmem_call(kernel, [f32(RING, rows + EXTRA, width)], name, 2 * m * n * width, 0, [],
                     w_near, x_near, w_far, x_far, loss)[0]


def after(value, *others):
    return lax.optimization_barrier((value, *others))[0]


def ring_shift(value, axis, step):
    return lax.ppermute(value, axis, [(i, (i + step) % RING) for i in range(RING)])


def ring_split(value, axis, sign):
    pairs = []
    for i in range(RING):
        for core in range(2):
            target = (i + (sign if core == 0 else -sign)) % RING
            pairs.append((i * 2 + core, target * 2 + core))
    return lax.ppermute(value, (axis, "core"), pairs)


def swap(value, axis):
    return lax.ppermute(value, axis, [(0, 1), (1, 0)])


def ring_gather(value, axis, first_core, wait_for=None):
    one = ring_shift(value, axis, 1)
    three = ring_shift(value, axis, 3)
    two = ring_split(jnp.where(first_core, one, three if wait_for is None else after(three, wait_for)), axis, 1)
    return [value, one, two, three]


def summed(own, other):
    return own + other.astype(jnp.float32)


def ring_outgoing(one, three, through, first_core):
    through = through.astype(jnp.float32)
    left = one + jnp.where(first_core, through, 0.0)
    right = three + jnp.where(first_core, 0.0, through)
    return left.astype(jnp.float16), right.astype(jnp.float16)


def ring_arrived(own, left, right, axis):
    return own + ring_shift(left, axis, -1).astype(jnp.float32) + ring_shift(right, axis, 1).astype(jnp.float32)


def on_device(image, text, log_scale):
    inverse_temp = jnp.exp(log_scale)
    rows = image.shape[0]
    core = lax.axis_index("core")
    place = [lax.axis_index(axis).reshape(1) for axis in AXES]
    scale = (inverse_temp * jnp.float32(math.log2(math.e))).reshape(1)
    image, text, scale, place, first_core = lax.optimization_barrier((image, text, scale, place, core == 0))

    text_far = swap(text, "ylo")
    image_far = swap(image, "yhi")
    text_near_slots = ring_gather(text, "z", first_core)
    text_near = join_call(text_near_slots, "join_text")
    text_far_slots = ring_gather(text_far, "z", first_core, text_near)
    image_near_slots = ring_gather(image, "x", first_core)
    image_far_slots = ring_gather(image_far, "x", first_core)
    image_near = join_call(image_near_slots, "join_image")
    image_near_other = swap(image_near, "core")
    image_far_other = [swap(a, "core") for a in image_far_slots]

    s_near, x_near, row_stat, col_stat, t_all = score_call(
        [image_near, image_near_other], [text_near] + text_far_slots, scale, place, 0, [], rows, "score_near")
    s_far, x_far, row_stat, col_stat = score_call(
        image_far_slots + image_far_other, [t_all], scale, place, 1, [row_stat, col_stat], rows, "score_far")

    loss_scale = math.log(2.0) / (2 * 128 * rows)
    one, two, three = (functools.partial(turned, step=step) for step in (1, 2, 3))
    cores, pairs = functools.partial(swapped, group=RING), functools.partial(swapped, group=2 * RING)
    row_stat, col_stat = merge_call(
        row_stat, [(swap(row_stat, "core"), cores)],
        col_stat, [(ring_shift(col_stat, "z", 1), one)], (None, None), "merge_core")
    row_stat, col_stat = merge_call(
        row_stat, [(ring_shift(row_stat, "x", 1), one), (ring_shift(row_stat, "x", 2), two),
                   (ring_shift(row_stat, "x", 3), three)],
        col_stat, [(ring_shift(col_stat, "z", 2), two)], (None, None), "merge_ring")
    row_lse, row_loss, col_lse, col_loss = merge_call(
        row_stat, [(swap(row_stat, "yhi"), pairs)],
        col_stat, [(swap(col_stat, "ylo"), cores)], (loss_scale, loss_scale), "merge_pair")

    w_far, far_own, far_part = image_call(s_far, row_lse, col_lse, col_loss, place, 1, t_all, rows, "image_far")
    far_send = far_part.astype(jnp.float16)
    far_other = swap(far_send, "core")
    w_near, near_own, near_part = image_call(
        s_near, after(row_lse, far_send), col_lse, col_loss, place, 0, t_all, rows, "image_near")
    near_send = near_part.astype(jnp.float16)
    near_other = swap(near_send, "core")
    far_text = text_call(w_near, x_near, w_far, x_far, after(row_loss, near_send), RING, rows, "text_far")
    far_text_two = far_text[2].astype(jnp.float16)
    far_text_through = ring_split(far_text_two, "z", -1)
    other, _ = lax.optimization_barrier(((near_other, far_other), far_text_two))
    near_other, far_other = other
    image_two = jnp.stack([summed(near_own[2], near_other[2]), summed(far_own[2], far_other[2])]).astype(jnp.float16)
    image_through = ring_split(image_two, "x", -1)
    near_text = text_call(w_near, x_near, w_far, x_far, after(row_loss, image_two), 0, rows, "text_near")
    near_text_two = near_text[2].astype(jnp.float16)
    near_text_through = ring_split(near_text_two, "z", -1)

    text_left, text_right = ring_outgoing(
        far_text[1], far_text[3], after(far_text_through, near_text_two), first_core)
    far_left, far_right = ring_outgoing(
        summed(far_own[1], far_other[1]), summed(far_own[3], far_other[3]), after(image_through, text_left)[1], first_core)
    near_text_left, near_text_right = ring_outgoing(
        near_text[1], near_text[3], after(near_text_through, far_left), first_core)
    near_left, near_right = ring_outgoing(
        summed(near_own[1], near_other[1]), summed(near_own[3], near_other[3]),
        after(image_through, near_text_left)[0], first_core)
    text_far_sum = ring_arrived(after(far_text[0], near_left), text_left, text_right, "z").astype(jnp.float16)
    text_far_in = swap(text_far_sum, "ylo")
    image_far_sum = ring_arrived(
        summed(far_own[0], after(far_other, text_far_sum)[0]), far_left, far_right, "x").astype(jnp.float16)
    image_far_in = swap(image_far_sum, "yhi")
    image_sum = (ring_arrived(summed(near_own[0], after(near_other, image_far_sum)[0]), near_left, near_right, "x")
                 + image_far_in.astype(jnp.float32))
    text_sum = (ring_arrived(near_text[0], near_text_left, near_text_right, "z")
                + text_far_in.astype(jnp.float32))

    digits = text_sum[rows:, 0] + image_sum[rows:, 0]
    loss_value = sum(digits[k] * unit for k, unit in enumerate(UNITS))
    return loss_value, inverse_temp * image_sum[:rows], inverse_temp * text_sum[:rows]


def solution(mesh):
    fine = Mesh(mesh.devices.reshape(2, 4, 4, 2, 2), AXES)
    text_spec = P(("yhi", "core", "ylo", "z", "x"), None)
    return jax.shard_map(
        on_device, mesh=fine, in_specs=(P(AXES, None), text_spec, P()),
        out_specs=(P(), P(AXES, None), text_spec), check_vma=False
    )
```

```python
import functools
import math

import jax
import jax.numpy as jnp
from jax import lax
from jax.experimental import pallas as pl
from jax.experimental.pallas import tpu as pltpu
from jax.sharding import Mesh, PartitionSpec as P

AXES = ("ylo", "z", "x", "yhi", "core")
RING = 4
TILE_SLOTS = 2
EXTRA = 8
UNITS = (256.0, 1.0, 2.0 ** -8, 2.0 ** -16, 2.0 ** -24)
VMEM_LIMIT = 12 * 1024 * 1024


def f32(*shape):
    return jax.ShapeDtypeStruct(shape, jnp.float32)


def bf16(*shape):
    return jax.ShapeDtypeStruct(shape, jnp.bfloat16)


def vmem_call(kernel, out_shape, name, flops, transcendentals, scalars, *args):
    vmem = pl.BlockSpec(memory_space=pltpu.VMEM)
    nbytes = sum(a.size * a.dtype.itemsize for a in args)
    nbytes += sum(math.prod(o.shape) * o.dtype.itemsize for o in out_shape)
    return pl.pallas_call(
        kernel,
        in_specs=[pl.BlockSpec(memory_space=pltpu.SMEM)] * len(scalars) + [vmem] * len(args),
        out_specs=[vmem] * len(out_shape),
        out_shape=out_shape,
        compiler_params=pltpu.CompilerParams(vmem_limit_bytes=VMEM_LIMIT),
        cost_estimate=pl.CostEstimate(flops=flops, bytes_accessed=nbytes, transcendentals=transcendentals),
        name=name,
    )(*scalars, *args)


def to_lanes(column):
    return jnp.broadcast_to(column, (column.shape[0], 128)).T[0:1, :]


def to_rows(line):
    return jnp.broadcast_to(line, (128, line.shape[1])).T[:, 0:1]


def merge(stats):
    top = stats[0][0]
    for stat in stats[1:]:
        top = jnp.maximum(top, stat[0])
    total = sum(stat[1] * jnp.exp2(stat[0] - top) for stat in stats)
    return [top, total] + [sum(stat[k] for stat in stats) for k in range(2, len(stats[0]))]


def place_refs(refs):
    return {axis: refs[k][0] for k, axis in enumerate(AXES)}


def image_block(place, h, slot):
    x = lax.rem(place["x"] + RING - slot % RING, RING)
    core = place["core"] if slot < RING else 1 - place["core"]
    yhi = place["yhi"] if h == 0 else 1 - place["yhi"]
    return ((place["ylo"] * 4 + place["z"]) * 4 + x) * 4 + yhi * 2 + core


def text_block(place, slot):
    z = lax.rem(place["z"] + RING - slot % RING, RING)
    ylo = place["ylo"] if slot < RING else 1 - place["ylo"]
    return (place["yhi"] * 2 + place["core"]) * 32 + (ylo * 4 + z) * 4 + place["x"]


def score_call(images, texts, scale, place, h, near_stats, rows, name):
    width = images[0].shape[1]
    sizes = [a.shape[0] for a in images]
    text_sizes = [a.shape[0] for a in texts]
    m, n = sum(sizes), sum(text_sizes)
    slots = m // rows
    before = near_stats[0].shape[1] if near_stats else 0
    keep_text = len(texts) > 1

    def kernel(scale_ref, *refs):
        place, refs = place_refs(refs), refs[len(AXES):]
        image_refs, refs = refs[:len(images)], refs[len(images):]
        text_refs, refs = refs[:len(texts)], refs[len(texts):]
        held, refs = refs[:len(near_stats)], refs[len(near_stats):]
        s_ref, x_ref, row_ref, col_ref = refs[:4]
        t_ref = refs[4] if keep_text else text_refs[0]

        def fill(target, sources, counts):
            at = 0
            for source, count in zip(sources, counts):
                target[pl.ds(at, count), :] = source[...]
                at += count

        if keep_text:
            fill(t_ref, text_refs, text_sizes)
        fill(x_ref, image_refs, sizes)
        tile = rows * TILE_SLOTS
        tiles = m // tile
        scale = scale_ref[0]
        col_parts = []

        def scores(i):
            s_ref[pl.ds(i * tile, tile), :] = scale * lax.dot_general(
                x_ref[pl.ds(i * tile, tile), :], t_ref[...], (((1,), (1,)), ((), ())),
                preferred_element_type=jnp.float32)

        def stats(i):
            s = s_ref[pl.ds(i * tile, tile), :]
            col_top = jnp.max(s, axis=0, keepdims=True)
            col_parts.append((col_top, jnp.sum(jnp.exp2(s - col_top), axis=0, keepdims=True)))
            for j in range(TILE_SLOTS):
                slot = i * TILE_SLOTS + j
                s = s_ref[pl.ds(slot * rows, rows), :]
                row_top = jnp.max(s, axis=1, keepdims=True)
                row_sum = jnp.sum(jnp.exp2(s - row_top), axis=1, keepdims=True)
                row_ref[0, pl.ds(before + slot, 1), :] = to_lanes(row_top)
                row_ref[1, pl.ds(before + slot, 1), :] = to_lanes(row_sum)

        scores(0)
        for i in range(tiles):
            if i + 1 < tiles:
                scores(i + 1)
            stats(i)
        top, total = merge(col_parts)
        for k in range(n // rows):
            at = slice(k * rows, (k + 1) * rows)
            part = [(top[:, at], total[:, at])]
            if held:
                part.append((held[1][0, pl.ds(k, 1), :], held[1][1, pl.ds(k, 1), :]))
            col_ref[0, pl.ds(k, 1), :], col_ref[1, pl.ds(k, 1), :] = merge(part)
        if held:
            row_ref[:, pl.ds(0, before), :] = held[0][...]
        row_ref[2, pl.ds(before, slots), :] = jnp.zeros((slots, rows), jnp.float32)
        for slot in range(slots):
            for k in range(n // rows):
                @pl.when(image_block(place, h, slot) == text_block(place, k))
                def _():
                    s = s_ref[pl.ds(slot * rows, rows), :][:, k * rows:(k + 1) * rows]
                    mask = (lax.broadcasted_iota(jnp.int32, (rows, 1), 0)
                            == lax.broadcasted_iota(jnp.int32, (1, rows), 1))
                    row_ref[2, pl.ds(before + slot, 1), :] = jnp.sum(jnp.where(mask, s, 0.0), axis=0, keepdims=True)

    out_shape = [f32(m, n), bf16(m, width), f32(3, before + slots, rows), f32(2, n // rows, rows)]
    out_shape += [bf16(n, width)] * keep_text
    return vmem_call(kernel, out_shape, name, 2 * m * n * width, 2 * m * n, [scale, *place],
                     *images, *texts, *near_stats)


def turned(ref, k, step):
    rings = []
    for lo in range(0, ref.shape[1], RING):
        rings.append(ref[k, pl.ds(lo + RING - step, step), :])
        rings.append(ref[k, pl.ds(lo, RING - step), :])
    return jnp.concatenate(rings, axis=0)


def swapped(ref, k, group):
    parts = []
    for lo in range(0, ref.shape[1], 2 * group):
        parts.append(ref[k, pl.ds(lo + group, group), :])
        parts.append(ref[k, pl.ds(lo, group), :])
    return jnp.concatenate(parts, axis=0)


def merge_call(row, row_in, col, col_in, loss_scale, name):
    arrays, out_shape = [], []
    for stat, came, scale in zip((row, col), (row_in, col_in), loss_scale):
        arrays += [stat] + [array for array, _ in came]
        out_shape += [f32(*stat.shape)] if scale is None else [f32(*stat.shape[1:]), f32(1, stat.shape[2])]

    def kernel(*refs):
        ins, outs = list(refs[:len(arrays)]), list(refs[len(arrays):])
        for stat, came, scale in zip((row, col), (row_in, col_in), loss_scale):
            planes = range(stat.shape[0])
            own = ins.pop(0)
            stats = [[own[p] for p in planes]]
            for _, order in came:
                ref = ins.pop(0)
                stats.append([order(ref, p) for p in planes])
            merged = merge(stats)
            if scale is None:
                out = outs.pop(0)
                for p in planes:
                    out[p] = merged[p]
            else:
                lse = merged[0] + jnp.log2(merged[1])
                outs.pop(0)[...] = lse
                diag = 2.0 * merged[2] if len(merged) > 2 else 0.0
                outs.pop(0)[...] = jnp.sum(lse - diag, axis=0, keepdims=True) * scale

    return vmem_call(kernel, out_shape, name, 0, 0, [], *arrays)


def join_call(parts, name):
    def kernel(*refs):
        at = 0
        for ref in refs[:-1]:
            refs[-1][pl.ds(at, ref.shape[0]), :] = ref[...]
            at += ref.shape[0]

    return vmem_call(kernel, [bf16(sum(p.shape[0] for p in parts), parts[0].shape[1])], name, 0, 0, [], *parts)[0]


def soft_weights(v, row_lse, col_lse, first_id, col_ids):
    ids = first_id + lax.broadcasted_iota(jnp.int32, (v.shape[0], 1), 0)
    soft = 0.5 * (jnp.exp2(v - to_rows(row_lse)) + jnp.exp2(v - col_lse))
    return (soft - jnp.where(ids == col_ids, 1.0, 0.0)).astype(jnp.bfloat16)


def weight_steps(w_ref, s_ref, row_ref, col_ref, place, h, rows):
    slots = range(col_ref.shape[0])
    col_lse = jnp.concatenate([col_ref[pl.ds(k, 1), :] for k in slots], axis=1)
    within = lax.broadcasted_iota(jnp.int32, (1, rows), 1)
    col_ids = jnp.concatenate([text_block(place, k) * rows + within for k in slots], axis=1)
    first = h * 2 * RING

    def weights(i):
        for j in range(TILE_SLOTS):
            slot = i * TILE_SLOTS + j
            at = pl.ds(slot * rows, rows)
            w_ref[at, :] = soft_weights(
                s_ref[at, :], row_ref[pl.ds(first + slot, 1), :], col_lse, image_block(place, h, slot) * rows, col_ids)

    return weights


def put_digits(part_ref, loss_ref, rows):
    left = jnp.sum(loss_ref[...], axis=1, keepdims=True)
    number = lax.broadcasted_iota(jnp.int32, (EXTRA, 1), 0)
    block = jnp.zeros((EXTRA, 1), jnp.float32)
    for k, unit in enumerate(UNITS):
        digit = jnp.floor(left * (1.0 / unit) + 0.5)
        left = left - digit * unit
        block = jnp.where(number == k, digit, block)
    for slot in range(part_ref.shape[0]):
        part_ref[slot, pl.ds(rows, EXTRA), :] = jnp.broadcast_to(block, (EXTRA, part_ref.shape[2]))


def put_slots(own_ref, other_ref, slot, part, rows):
    for j in range(part.shape[0] // rows):
        out = own_ref if slot + j < RING else other_ref
        out[(slot + j) % RING, pl.ds(0, rows), :] = part[j * rows:(j + 1) * rows]


def image_call(s, row_lse, col_lse, loss, place, h, text, rows, name):
    m, n = s.shape
    width = text.shape[1]

    def kernel(*refs):
        place, refs = place_refs(refs), refs[len(AXES):]
        s_ref, row_ref, col_ref, loss_ref, t_ref, w_ref, own_ref, other_ref = refs
        tile = rows * TILE_SLOTS
        tiles = m // tile
        weights = weight_steps(w_ref, s_ref, row_ref, col_ref, place, h, rows)
        put_digits(own_ref, loss_ref, rows)
        other_ref[:, pl.ds(rows, EXTRA), :] = own_ref[:, pl.ds(rows, EXTRA), :]

        def dots(i):
            put_slots(own_ref, other_ref, i * TILE_SLOTS, jnp.dot(
                w_ref[pl.ds(i * tile, tile), :], t_ref[...], preferred_element_type=jnp.float32), rows)

        weights(0)
        for i in range(tiles):
            if i + 1 < tiles:
                weights(i + 1)
            dots(i)

    parts = [f32(RING, rows + EXTRA, width)] * 2
    return vmem_call(kernel, [bf16(m, n)] + parts, name, 2 * m * n * width, 2 * m * n,
                     place, s, row_lse, col_lse, loss, text)


def text_columns(first, n, rows):
    lo = first * rows // 128 * 128
    hi = min(n, -(-(first + RING) * rows // 128) * 128)
    return pl.ds(lo, hi - lo), first * rows - lo


def text_call(w_near, x_near, w_far, x_far, loss, first, rows, name):
    m, n = w_near.shape
    width = x_near.shape[1]
    chunk = width

    def kernel(wn_ref, xn_ref, wf_ref, xf_ref, loss_ref, part_ref):
        dims = (((0,), (0,)), ((), ()))
        columns, lead = text_columns(first, n, rows)
        put_digits(part_ref, loss_ref, rows)
        for j in range(width // chunk):
            at = pl.ds(j * chunk, chunk)
            part = (lax.dot_general(wf_ref[:, columns], xf_ref[:, at], dims, preferred_element_type=jnp.float32)
                    + lax.dot_general(wn_ref[:, columns], xn_ref[:, at], dims, preferred_element_type=jnp.float32))
            for k in range(RING):
                part_ref[k, pl.ds(0, rows), at] = part[lead + k * rows:lead + (k + 1) * rows]

    return vmem_call(kernel, [f32(RING, rows + EXTRA, width)], name, 2 * m * n * width, 0, [],
                     w_near, x_near, w_far, x_far, loss)[0]


def after(value, *others):
    return lax.optimization_barrier((value, *others))[0]


def ring_shift(value, axis, step):
    return lax.ppermute(value, axis, [(i, (i + step) % RING) for i in range(RING)])


def ring_split(value, axis, sign):
    pairs = []
    for i in range(RING):
        for core in range(2):
            target = (i + (sign if core == 0 else -sign)) % RING
            pairs.append((i * 2 + core, target * 2 + core))
    return lax.ppermute(value, (axis, "core"), pairs)


def swap(value, axis):
    return lax.ppermute(value, axis, [(0, 1), (1, 0)])


def ring_gather(value, axis, first_core, wait_for=None):
    one = ring_shift(value, axis, 1)
    three = ring_shift(value, axis, 3)
    two = ring_split(jnp.where(first_core, one, three if wait_for is None else after(three, wait_for)), axis, 1)
    return [value, one, two, three]


def summed(own, other):
    return own + other.astype(jnp.float32)


def ring_outgoing(one, three, through, first_core):
    through = through.astype(jnp.float32)
    left = one + jnp.where(first_core, through, 0.0)
    right = three + jnp.where(first_core, 0.0, through)
    return left.astype(jnp.float16), right.astype(jnp.float16)


def ring_arrived(own, left, right, axis):
    return own + ring_shift(left, axis, -1).astype(jnp.float32) + ring_shift(right, axis, 1).astype(jnp.float32)


def on_device(image, text, log_scale):
    inverse_temp = jnp.exp(log_scale)
    rows = image.shape[0]
    core = lax.axis_index("core")
    place = [lax.axis_index(axis).reshape(1) for axis in AXES]
    scale = (inverse_temp * jnp.float32(math.log2(math.e))).reshape(1)
    image, text, scale, place, first_core = lax.optimization_barrier((image, text, scale, place, core == 0))

    text_far = swap(text, "ylo")
    image_far = swap(image, "yhi")
    text_near_slots = ring_gather(text, "z", first_core)
    text_near = join_call(text_near_slots, "join_text")
    text_far_slots = ring_gather(text_far, "z", first_core, text_near)
    image_near_slots = ring_gather(image, "x", first_core)
    image_far_slots = ring_gather(image_far, "x", first_core)
    image_near = join_call(image_near_slots, "join_image")
    image_near_other = swap(image_near, "core")
    image_far_other = [swap(a, "core") for a in image_far_slots]

    s_near, x_near, row_stat, col_stat, t_all = score_call(
        [image_near, image_near_other], [text_near] + text_far_slots, scale, place, 0, [], rows, "score_near")
    s_far, x_far, row_stat, col_stat = score_call(
        image_far_slots + image_far_other, [t_all], scale, place, 1, [row_stat, col_stat], rows, "score_far")

    loss_scale = math.log(2.0) / (2 * 128 * rows)
    one, two, three = (functools.partial(turned, step=step) for step in (1, 2, 3))
    cores, pairs = functools.partial(swapped, group=RING), functools.partial(swapped, group=2 * RING)
    row_stat, col_stat = merge_call(
        row_stat, [(swap(row_stat, "core"), cores)],
        col_stat, [(ring_shift(col_stat, "z", 1), one)], (None, None), "merge_core")
    row_stat, col_stat = merge_call(
        row_stat, [(ring_shift(row_stat, "x", 1), one), (ring_shift(row_stat, "x", 2), two),
                   (ring_shift(row_stat, "x", 3), three)],
        col_stat, [(ring_shift(col_stat, "z", 2), two)], (None, None), "merge_ring")
    row_lse, row_loss, col_lse, col_loss = merge_call(
        row_stat, [(swap(row_stat, "yhi"), pairs)],
        col_stat, [(swap(col_stat, "ylo"), cores)], (loss_scale, loss_scale), "merge_pair")

    w_far, far_own, far_part = image_call(s_far, row_lse, col_lse, col_loss, place, 1, t_all, rows, "image_far")
    far_send = far_part.astype(jnp.float16)
    far_other = swap(far_send, "core")
    w_near, near_own, near_part = image_call(
        s_near, after(row_lse, far_send), col_lse, col_loss, place, 0, t_all, rows, "image_near")
    near_send = near_part.astype(jnp.float16)
    near_other = swap(near_send, "core")
    far_text = text_call(w_near, x_near, w_far, x_far, after(row_loss, near_send), RING, rows, "text_far")
    far_text_two = far_text[2].astype(jnp.float16)
    far_text_through = ring_split(far_text_two, "z", -1)
    other, _ = lax.optimization_barrier(((near_other, far_other), far_text_two))
    near_other, far_other = other
    image_two = jnp.stack([summed(near_own[2], near_other[2]), summed(far_own[2], far_other[2])]).astype(jnp.float16)
    image_through = ring_split(image_two, "x", -1)
    near_text = text_call(w_near, x_near, w_far, x_far, after(row_loss, image_two), 0, rows, "text_near")
    near_text_two = near_text[2].astype(jnp.float16)
    near_text_through = ring_split(near_text_two, "z", -1)

    text_left, text_right = ring_outgoing(
        far_text[1], far_text[3], after(far_text_through, near_text_two), first_core)
    far_left, far_right = ring_outgoing(
        summed(far_own[1], far_other[1]), summed(far_own[3], far_other[3]), after(image_through, text_left)[1], first_core)
    near_text_left, near_text_right = ring_outgoing(
        near_text[1], near_text[3], after(near_text_through, far_left), first_core)
    near_left, near_right = ring_outgoing(
        summed(near_own[1], near_other[1]), summed(near_own[3], near_other[3]),
        after(image_through, near_text_left)[0], first_core)
    text_far_sum = ring_arrived(after(far_text[0], near_left), text_left, text_right, "z").astype(jnp.float16)
    text_far_in = swap(text_far_sum, "ylo")
    image_far_sum = ring_arrived(
        summed(far_own[0], after(far_other, text_far_sum)[0]), far_left, far_right, "x").astype(jnp.float16)
    image_far_in = swap(image_far_sum, "yhi")
    image_terms = [near_own[0], after(near_other, image_far_sum)[0], ring_shift(near_left, "x", -1),
                   ring_shift(near_right, "x", 1), image_far_in]
    text_terms = [near_text[0], ring_shift(near_text_left, "z", -1), ring_shift(near_text_right, "z", 1), text_far_in]
    image_grad, text_grad = (
        inverse_temp * sum(term[:rows].astype(jnp.float32) for term in terms) for terms in (image_terms, text_terms))
    digits = sum(term[rows:, 0].astype(jnp.float32) for term in text_terms + image_terms)
    loss_value = sum(digits[k] * unit for k, unit in enumerate(UNITS))
    return loss_value, image_grad, text_grad


def solution(mesh):
    fine = Mesh(mesh.devices.reshape(2, 4, 4, 2, 2), AXES)
    text_spec = P(("yhi", "core", "ylo", "z", "x"), None)
    return jax.shard_map(
        on_device, mesh=fine, in_specs=(P(AXES, None), text_spec, P()),
        out_specs=(P(), P(AXES, None), text_spec), check_vma=False
    )
```

```python
import functools
import math

import jax
import jax.numpy as jnp
from jax import lax
from jax.experimental import pallas as pl
from jax.experimental.pallas import tpu as pltpu
from jax.sharding import Mesh, PartitionSpec as P

AXES = ("ylo", "z", "x", "yhi", "core")
RING = 4
TILE_SLOTS = 2
EXTRA = 8
UNITS = (256.0, 1.0, 2.0 ** -8, 2.0 ** -16, 2.0 ** -24)
VMEM_LIMIT = 12 * 1024 * 1024


def f32(*shape):
    return jax.ShapeDtypeStruct(shape, jnp.float32)


def bf16(*shape):
    return jax.ShapeDtypeStruct(shape, jnp.bfloat16)


def vmem_call(kernel, out_shape, name, flops, transcendentals, scalars, *args):
    vmem = pl.BlockSpec(memory_space=pltpu.VMEM)
    nbytes = sum(a.size * a.dtype.itemsize for a in args)
    nbytes += sum(math.prod(o.shape) * o.dtype.itemsize for o in out_shape)
    return pl.pallas_call(
        kernel,
        in_specs=[pl.BlockSpec(memory_space=pltpu.SMEM)] * len(scalars) + [vmem] * len(args),
        out_specs=[vmem] * len(out_shape),
        out_shape=out_shape,
        compiler_params=pltpu.CompilerParams(vmem_limit_bytes=VMEM_LIMIT),
        cost_estimate=pl.CostEstimate(flops=flops, bytes_accessed=nbytes, transcendentals=transcendentals),
        name=name,
    )(*scalars, *args)


def to_lanes(column):
    return jnp.broadcast_to(column, (column.shape[0], 128)).T[0:1, :]


def to_rows(line):
    return jnp.broadcast_to(line, (128, line.shape[1])).T[:, 0:1]


def merge(stats):
    top = stats[0][0]
    for stat in stats[1:]:
        top = jnp.maximum(top, stat[0])
    total = sum(stat[1] * jnp.exp2(stat[0] - top) for stat in stats)
    return [top, total] + [sum(stat[k] for stat in stats) for k in range(2, len(stats[0]))]


def place_refs(refs):
    return {axis: refs[k][0] for k, axis in enumerate(AXES)}


def image_block(place, h, slot):
    x = lax.rem(place["x"] + RING - slot % RING, RING)
    core = place["core"] if slot < RING else 1 - place["core"]
    yhi = place["yhi"] if h == 0 else 1 - place["yhi"]
    return ((place["ylo"] * 4 + place["z"]) * 4 + x) * 4 + yhi * 2 + core


def text_block(place, slot):
    z = lax.rem(place["z"] + RING - slot % RING, RING)
    ylo = place["ylo"] if slot < RING else 1 - place["ylo"]
    return (place["yhi"] * 2 + place["core"]) * 32 + (ylo * 4 + z) * 4 + place["x"]


def score_call(images, texts, scale, place, h, near_stats, rows, name):
    width = images[0].shape[1]
    sizes = [a.shape[0] for a in images]
    text_sizes = [a.shape[0] for a in texts]
    m, n = sum(sizes), sum(text_sizes)
    slots = m // rows
    before = near_stats[0].shape[1] if near_stats else 0
    keep_text = len(texts) > 1

    def kernel(scale_ref, *refs):
        place, refs = place_refs(refs), refs[len(AXES):]
        image_refs, refs = refs[:len(images)], refs[len(images):]
        text_refs, refs = refs[:len(texts)], refs[len(texts):]
        held, refs = refs[:len(near_stats)], refs[len(near_stats):]
        s_ref, x_ref, row_ref, col_ref = refs[:4]
        t_ref = refs[4] if keep_text else text_refs[0]

        def fill(target, sources, counts):
            at = 0
            for source, count in zip(sources, counts):
                target[pl.ds(at, count), :] = source[...]
                at += count

        if keep_text:
            fill(t_ref, text_refs, text_sizes)
        fill(x_ref, image_refs, sizes)
        tile = rows * TILE_SLOTS
        tiles = m // tile
        scale = scale_ref[0]
        col_parts = []

        def scores(i):
            s_ref[pl.ds(i * tile, tile), :] = scale * lax.dot_general(
                x_ref[pl.ds(i * tile, tile), :], t_ref[...], (((1,), (1,)), ((), ())),
                preferred_element_type=jnp.float32)

        def stats(i):
            s = s_ref[pl.ds(i * tile, tile), :]
            col_top = jnp.max(s, axis=0, keepdims=True)
            col_parts.append((col_top, jnp.sum(jnp.exp2(s - col_top), axis=0, keepdims=True)))
            for j in range(TILE_SLOTS):
                slot = i * TILE_SLOTS + j
                s = s_ref[pl.ds(slot * rows, rows), :]
                row_top = jnp.max(s, axis=1, keepdims=True)
                row_sum = jnp.sum(jnp.exp2(s - row_top), axis=1, keepdims=True)
                row_ref[0, pl.ds(before + slot, 1), :] = to_lanes(row_top)
                row_ref[1, pl.ds(before + slot, 1), :] = to_lanes(row_sum)

        scores(0)
        for i in range(tiles):
            if i + 1 < tiles:
                scores(i + 1)
            stats(i)
        top, total = merge(col_parts)
        for k in range(n // rows):
            at = slice(k * rows, (k + 1) * rows)
            part = [(top[:, at], total[:, at])]
            if held:
                part.append((held[1][0, pl.ds(k, 1), :], held[1][1, pl.ds(k, 1), :]))
            col_ref[0, pl.ds(k, 1), :], col_ref[1, pl.ds(k, 1), :] = merge(part)
        if held:
            row_ref[:, pl.ds(0, before), :] = held[0][...]
        row_ref[2, pl.ds(before, slots), :] = jnp.zeros((slots, rows), jnp.float32)
        for slot in range(slots):
            for k in range(n // rows):
                @pl.when(image_block(place, h, slot) == text_block(place, k))
                def _():
                    s = s_ref[pl.ds(slot * rows, rows), :][:, k * rows:(k + 1) * rows]
                    mask = (lax.broadcasted_iota(jnp.int32, (rows, 1), 0)
                            == lax.broadcasted_iota(jnp.int32, (1, rows), 1))
                    row_ref[2, pl.ds(before + slot, 1), :] = jnp.sum(jnp.where(mask, s, 0.0), axis=0, keepdims=True)

    out_shape = [f32(m, n), bf16(m, width), f32(3, before + slots, rows), f32(2, n // rows, rows)]
    out_shape += [bf16(n, width)] * keep_text
    return vmem_call(kernel, out_shape, name, 2 * m * n * width, 2 * m * n, [scale, *place],
                     *images, *texts, *near_stats)


def turned(ref, k, step):
    rings = []
    for lo in range(0, ref.shape[1], RING):
        rings.append(ref[k, pl.ds(lo + RING - step, step), :])
        rings.append(ref[k, pl.ds(lo, RING - step), :])
    return jnp.concatenate(rings, axis=0)


def swapped(ref, k, group):
    parts = []
    for lo in range(0, ref.shape[1], 2 * group):
        parts.append(ref[k, pl.ds(lo + group, group), :])
        parts.append(ref[k, pl.ds(lo, group), :])
    return jnp.concatenate(parts, axis=0)


def merge_call(row, row_in, col, col_in, loss_scale, name):
    arrays, out_shape = [], []
    for stat, came, scale in zip((row, col), (row_in, col_in), loss_scale):
        arrays += [stat] + [array for array, _ in came]
        out_shape += [f32(*stat.shape)] if scale is None else [f32(*stat.shape[1:]), f32(1, stat.shape[2])]

    def kernel(*refs):
        ins, outs = list(refs[:len(arrays)]), list(refs[len(arrays):])
        for stat, came, scale in zip((row, col), (row_in, col_in), loss_scale):
            planes = range(stat.shape[0])
            own = ins.pop(0)
            stats = [[own[p] for p in planes]]
            for _, order in came:
                ref = ins.pop(0)
                stats.append([order(ref, p) for p in planes])
            merged = merge(stats)
            if scale is None:
                out = outs.pop(0)
                for p in planes:
                    out[p] = merged[p]
            else:
                lse = merged[0] + jnp.log2(merged[1])
                outs.pop(0)[...] = lse
                diag = 2.0 * merged[2] if len(merged) > 2 else 0.0
                outs.pop(0)[...] = jnp.sum(lse - diag, axis=0, keepdims=True) * scale

    return vmem_call(kernel, out_shape, name, 0, 0, [], *arrays)


def join_call(parts, name):
    def kernel(*refs):
        at = 0
        for ref in refs[:-1]:
            refs[-1][pl.ds(at, ref.shape[0]), :] = ref[...]
            at += ref.shape[0]

    return vmem_call(kernel, [bf16(sum(p.shape[0] for p in parts), parts[0].shape[1])], name, 0, 0, [], *parts)[0]


def soft_weights(v, row_lse, col_lse, first_id, col_ids):
    ids = first_id + lax.broadcasted_iota(jnp.int32, (v.shape[0], 1), 0)
    soft = 0.5 * (jnp.exp2(v - to_rows(row_lse)) + jnp.exp2(v - col_lse))
    return (soft - jnp.where(ids == col_ids, 1.0, 0.0)).astype(jnp.bfloat16)


def weight_steps(w_ref, s_ref, row_ref, col_ref, place, h, rows):
    slots = range(col_ref.shape[0])
    col_lse = jnp.concatenate([col_ref[pl.ds(k, 1), :] for k in slots], axis=1)
    within = lax.broadcasted_iota(jnp.int32, (1, rows), 1)
    col_ids = jnp.concatenate([text_block(place, k) * rows + within for k in slots], axis=1)
    first = h * 2 * RING

    def weights(i):
        for j in range(TILE_SLOTS):
            slot = i * TILE_SLOTS + j
            at = pl.ds(slot * rows, rows)
            w_ref[at, :] = soft_weights(
                s_ref[at, :], row_ref[pl.ds(first + slot, 1), :], col_lse, image_block(place, h, slot) * rows, col_ids)

    return weights


def put_digits(part_ref, loss_ref, rows):
    left = jnp.sum(loss_ref[...], axis=1, keepdims=True)
    number = lax.broadcasted_iota(jnp.int32, (EXTRA, 1), 0)
    block = jnp.zeros((EXTRA, 1), jnp.float32)
    for k, unit in enumerate(UNITS):
        digit = jnp.floor(left * (1.0 / unit) + 0.5)
        left = left - digit * unit
        block = jnp.where(number == k, digit, block)
    for slot in range(part_ref.shape[0]):
        part_ref[slot, pl.ds(rows, EXTRA), :] = jnp.broadcast_to(block, (EXTRA, part_ref.shape[2]))


def put_slots(own_ref, other_ref, slot, part, rows):
    for j in range(part.shape[0] // rows):
        out = own_ref if slot + j < RING else other_ref
        out[(slot + j) % RING, pl.ds(0, rows), :] = part[j * rows:(j + 1) * rows]


def image_call(s, row_lse, col_lse, loss, place, h, text, rows, name):
    m, n = s.shape
    width = text.shape[1]

    def kernel(*refs):
        place, refs = place_refs(refs), refs[len(AXES):]
        s_ref, row_ref, col_ref, loss_ref, t_ref, w_ref, own_ref, other_ref = refs
        tile = rows * TILE_SLOTS
        tiles = m // tile
        weights = weight_steps(w_ref, s_ref, row_ref, col_ref, place, h, rows)
        put_digits(own_ref, loss_ref, rows)
        other_ref[:, pl.ds(rows, EXTRA), :] = own_ref[:, pl.ds(rows, EXTRA), :]

        def dots(i):
            put_slots(own_ref, other_ref, i * TILE_SLOTS, jnp.dot(
                w_ref[pl.ds(i * tile, tile), :], t_ref[...], preferred_element_type=jnp.float32), rows)

        weights(0)
        for i in range(tiles):
            if i + 1 < tiles:
                weights(i + 1)
            dots(i)

    parts = [f32(RING, rows + EXTRA, width)] * 2
    return vmem_call(kernel, [bf16(m, n)] + parts, name, 2 * m * n * width, 2 * m * n,
                     place, s, row_lse, col_lse, loss, text)


def text_columns(first, n, rows):
    lo = first * rows // 128 * 128
    hi = min(n, -(-(first + RING) * rows // 128) * 128)
    return pl.ds(lo, hi - lo), first * rows - lo


def text_call(w_near, x_near, w_far, x_far, loss, first, rows, name):
    m, n = w_near.shape
    width = x_near.shape[1]
    chunk = width

    def kernel(wn_ref, xn_ref, wf_ref, xf_ref, loss_ref, part_ref):
        dims = (((0,), (0,)), ((), ()))
        columns, lead = text_columns(first, n, rows)
        put_digits(part_ref, loss_ref, rows)
        for j in range(width // chunk):
            at = pl.ds(j * chunk, chunk)
            part = (lax.dot_general(wf_ref[:, columns], xf_ref[:, at], dims, preferred_element_type=jnp.float32)
                    + lax.dot_general(wn_ref[:, columns], xn_ref[:, at], dims, preferred_element_type=jnp.float32))
            for k in range(RING):
                part_ref[k, pl.ds(0, rows), at] = part[lead + k * rows:lead + (k + 1) * rows]

    return vmem_call(kernel, [f32(RING, rows + EXTRA, width)], name, 2 * m * n * width, 0, [],
                     w_near, x_near, w_far, x_far, loss)[0]


def after(value, *others):
    return lax.optimization_barrier((value, *others))[0]


def ring_shift(value, axis, step):
    return lax.ppermute(value, axis, [(i, (i + step) % RING) for i in range(RING)])


def ring_split(value, axis, sign):
    pairs = []
    for i in range(RING):
        for core in range(2):
            target = (i + (sign if core == 0 else -sign)) % RING
            pairs.append((i * 2 + core, target * 2 + core))
    return lax.ppermute(value, (axis, "core"), pairs)


def swap(value, axis):
    return lax.ppermute(value, axis, [(0, 1), (1, 0)])


def ring_gather(value, axis, first_core, wait_for=None):
    one = ring_shift(value, axis, 1)
    three = ring_shift(value, axis, 3)
    two = ring_split(jnp.where(first_core, one, three if wait_for is None else after(three, wait_for)), axis, 1)
    return [value, one, two, three]


def summed(own, other):
    return own + other.astype(jnp.float32)


def ring_outgoing(one, three, through, first_core):
    through = through.astype(jnp.float32)
    left = one + jnp.where(first_core, through, 0.0)
    right = three + jnp.where(first_core, 0.0, through)
    return left.astype(jnp.float16), right.astype(jnp.float16)


def ring_arrived(own, left, right, axis):
    return own + ring_shift(left, axis, -1).astype(jnp.float32) + ring_shift(right, axis, 1).astype(jnp.float32)


def on_device(image, text, log_scale):
    inverse_temp = jnp.exp(log_scale)
    rows = image.shape[0]
    core = lax.axis_index("core")
    place = [lax.axis_index(axis).reshape(1) for axis in AXES]
    scale = (inverse_temp * jnp.float32(math.log2(math.e))).reshape(1)
    image, text, scale, place, first_core = lax.optimization_barrier((image, text, scale, place, core == 0))

    text_far = swap(text, "ylo")
    image_far = swap(image, "yhi")
    text_near_slots = ring_gather(text, "z", first_core)
    text_near = join_call(text_near_slots, "join_text")
    text_far_slots = ring_gather(text_far, "z", first_core, text_near)
    image_near_slots = ring_gather(image, "x", first_core)
    image_far_slots = ring_gather(image_far, "x", first_core)
    image_near = join_call(image_near_slots, "join_image")
    image_near_other = swap(image_near, "core")
    image_far_other = [swap(a, "core") for a in image_far_slots]

    s_near, x_near, row_stat, col_stat, t_all = score_call(
        [image_near, image_near_other], [text_near] + text_far_slots, scale, place, 0, [], rows, "score_near")
    s_far, x_far, row_stat, col_stat = score_call(
        image_far_slots + image_far_other, [t_all], scale, place, 1, [row_stat, col_stat], rows, "score_far")

    loss_scale = math.log(2.0) / (2 * 128 * rows)
    one, two, three = (functools.partial(turned, step=step) for step in (1, 2, 3))
    cores, pairs = functools.partial(swapped, group=RING), functools.partial(swapped, group=2 * RING)
    row_stat, col_stat = merge_call(
        row_stat, [(swap(row_stat, "core"), cores)],
        col_stat, [(ring_shift(col_stat, "z", 1), one)], (None, None), "merge_core")
    row_stat, col_stat = merge_call(
        row_stat, [(ring_shift(row_stat, "x", 1), one), (ring_shift(row_stat, "x", 2), two),
                   (ring_shift(row_stat, "x", 3), three)],
        col_stat, [(ring_shift(col_stat, "z", 2), two)], (None, None), "merge_ring")
    row_lse, row_loss, col_lse, col_loss = merge_call(
        row_stat, [(swap(row_stat, "yhi"), pairs)],
        col_stat, [(swap(col_stat, "ylo"), cores)], (loss_scale, loss_scale), "merge_pair")

    w_far, far_own, far_part = image_call(s_far, row_lse, col_lse, col_loss, place, 1, t_all, rows, "image_far")
    far_send = far_part.astype(jnp.float16)
    far_other = swap(far_send, "core")
    w_near, near_own, near_part = image_call(
        s_near, after(row_lse, far_send), col_lse, col_loss, place, 0, t_all, rows, "image_near")
    near_send = near_part.astype(jnp.float16)
    near_other = swap(near_send, "core")
    far_text = text_call(w_near, x_near, w_far, x_far, after(row_loss, near_send), RING, rows, "text_far")
    far_text_two = far_text[2].astype(jnp.float16)
    far_text_through = ring_split(far_text_two, "z", -1)
    other, _ = lax.optimization_barrier(((near_other, far_other), far_text_two))
    near_other, far_other = other
    image_two = jnp.stack([summed(near_own[2], near_other[2]), summed(far_own[2], far_other[2])]).astype(jnp.float16)
    image_through = ring_split(image_two, "x", -1)
    near_text = text_call(w_near, x_near, w_far, x_far, after(row_loss, image_two), 0, rows, "text_near")
    near_text_two = near_text[2].astype(jnp.float16)
    near_text_through = ring_split(near_text_two, "z", -1)

    text_left, text_right = ring_outgoing(
        far_text[1], far_text[3], after(far_text_through, near_text_two), first_core)
    far_left, far_right = ring_outgoing(
        summed(far_own[1], far_other[1]), summed(far_own[3], far_other[3]), after(image_through, text_left)[1], first_core)
    near_left, near_right = ring_outgoing(
        summed(near_own[1], near_other[1]), summed(near_own[3], near_other[3]),
        after(image_through, far_left)[0], first_core)
    text_far_sum = ring_arrived(after(far_text[0], near_left), text_left, text_right, "z").astype(jnp.float16)
    text_far_in = swap(text_far_sum, "ylo")
    image_far_sum = ring_arrived(
        summed(far_own[0], after(far_other, text_far_sum)[0]), far_left, far_right, "x").astype(jnp.float16)
    image_far_in = swap(image_far_sum, "yhi")
    near_text_left, near_text_right = ring_outgoing(
        near_text[1], near_text[3], after(near_text_through, image_far_sum), first_core)
    image_sum = (ring_arrived(summed(near_own[0], after(near_other, image_far_sum)[0]), near_left, near_right, "x")
                 + image_far_in.astype(jnp.float32))
    text_sum = (ring_arrived(near_text[0], near_text_left, near_text_right, "z")
                + text_far_in.astype(jnp.float32))

    digits = text_sum[rows:, 0] + image_sum[rows:, 0]
    loss_value = sum(digits[k] * unit for k, unit in enumerate(UNITS))
    return loss_value, inverse_temp * image_sum[:rows], inverse_temp * text_sum[:rows]


def solution(mesh):
    fine = Mesh(mesh.devices.reshape(2, 4, 4, 2, 2), AXES)
    text_spec = P(("yhi", "core", "ylo", "z", "x"), None)
    return jax.shard_map(
        on_device, mesh=fine, in_specs=(P(AXES, None), text_spec, P()),
        out_specs=(P(), P(AXES, None), text_spec), check_vma=False
    )
```
